512 devices in a mesh: energy: 64 (over y, x, core), space: 8 (over z).
Axes of the slice: x: 4, y: 8, z: 8, core: 2. Of those that a mesh axis runs over, the one named last changes fastest.
Arguments:
- inverses: float32 [128, 16, 256, 256], P('energy', 'space'), may hold values from -0.375 to 0.375
- coupling: float32 [16, 256, 256], P('space'), may hold values from -0.375 to 0.375
- source: float32 [128, 16, 256, 256], P('energy', 'space'), may hold values from -6 to 6
- screened: float32 [128, 4096, 256], P('energy', 'space'), may hold values from -0.12 to 0.12
- kept_rows: int32 [4096], P('space'), may hold values from 0 to 511
- live_count: int32 [8], P('space'), may hold values from 128 to 512, as said below
Outputs:
- sigma_kept: float32 [128, 4096, 256], P('energy', 'space')
The draws below stay inside these ranges and needn't reach their ends.
Inputs may be any that keep to these rules, and one draw needn't show every extreme that they name: `live_count`: between 128 and 512; some partition has exactly 512 live slots.
All inputs are finite; a program needn't handle non-finite values.
Results may differ from the reference program's by a relative error of at most 0.00021.
Values sent between devices are 32-bit elements; how exact they have to be, the bound alone decides.
No kernel may reach another device: no remote copies, remote signals or barrier semaphores. Data moves between devices by JAX's collectives and lax.ppermute only.
A program may use at most 64 MiB of HBM per device.

```python
import jax
import jax.numpy as jnp
from jax import lax

NB = 256
B_DEV = 2
KEEP = 512
NE = 128
NBLK = 16
N_SPACE = 8


def draw_live_count(key, part):
    key = jax.random.fold_in(key, 7)
    first, second = jax.random.split(key)
    counts = jax.random.randint(first, (N_SPACE,), KEEP // 4, KEEP + 1)
    where = jax.random.randint(second, (), 0, N_SPACE)
    return counts.at[where].set(KEEP).astype(jnp.int32)


def with_ends(array, rng, least, top_value):
    extent = array.shape
    spot = [jax.random.randint(jax.random.fold_in(rng, axis), (), 0, extent[axis]) for axis in range(len(extent))]
    array = array.at[tuple(spot)].set(least)
    longest = extent.index(max(extent))
    spot[longest] = (spot[longest] + 1) % extent[longest]
    return array.at[tuple(spot)].set(top_value)


def level_of(stream_key, dims, pieces, least, largest):
    factor_of, own = 1.0, jax.random.fold_in(stream_key, 6)
    for dim, parts in pieces:
        heights = jnp.exp(jax.random.uniform(jax.random.fold_in(own, dim), (parts,), jnp.float32, least / len(pieces), largest / len(pieces)))
        factor_of = factor_of * jnp.repeat(heights, dims[dim] // parts).reshape([-1 if axis == dim else 1 for axis in range(len(dims))])
    return factor_of


def normal_values(rng, extent, width, limit, cuts=(), kind=jnp.bfloat16):
    result = jax.random.normal(rng, extent, jnp.float32) * width
    if len(cuts) > 0:
        result = level_of(rng, extent, cuts, -0.22, 0.18) * result
    return jnp.clip(result, min=-limit, max=limit).astype(kind)


def setup_inputs(seed: int = 0) -> dict:
    arg_keys = jax.random.split(jax.random.key(seed), 7)
    inverses = normal_values(arg_keys[0], (NE, NBLK, NB, NB), NB ** -0.5, 0.375, ((0, 64), (1, 8)), jnp.float32)
    coupling = normal_values(arg_keys[1], (NBLK, NB, NB), (NB + NB // 20) ** -0.5, 0.375, ((0, 8),), jnp.float32)
    source = normal_values(arg_keys[2], (NE, NBLK, NB, NB), 1.0, 6.0, ((0, 64), (1, 8)), jnp.float32)
    screened = normal_values(arg_keys[3], (NE, N_SPACE * KEEP, NB), 0.02, 0.12, ((0, 64), (1, 8)), jnp.float32)
    kept_rows = with_ends(jax.random.randint(arg_keys[4], (N_SPACE * KEEP,), 0, B_DEV * NB), jax.random.fold_in(arg_keys[4], 1), 0, (B_DEV * NB) - 1).astype(jnp.int32)
    live_count = draw_live_count(jax.random.fold_in(arg_keys[6], 71), 0)
    return dict(inverses=inverses, coupling=coupling, source=source, screened=screened, kept_rows=kept_rows, live_count=live_count)


def mult(left, right):
    return jnp.matmul(left, right, precision=lax.Precision.HIGHEST)


def reference(inverses, coupling, source, screened, kept_rows, live_count):
    slots = jnp.arange(N_SPACE * KEEP, dtype=jnp.int32)
    owner = slots // KEEP
    global_rows = (owner * (B_DEV * NB) + kept_rows).astype(jnp.int32)
    live = ((slots % KEEP) < live_count[owner]).astype(jnp.float32)

    def one_energy(pair):
        inverse_blocks, source_blocks = pair
        transfer = mult(inverse_blocks, coupling)
        injected = mult(mult(inverse_blocks, source_blocks), jnp.swapaxes(inverse_blocks, -1, -2))

        def advance(state, item):
            step_map, step_add = item
            state = mult(mult(step_map, state), step_map.T) + step_add
            return state, state

        start = jnp.zeros((NB, NB), jnp.float32)
        _, stacked = lax.scan(advance, start, (transfer, injected))
        rows = stacked.reshape(NBLK * NB, NB)
        return jnp.take(rows, global_rows, axis=0) * live[:, None]

    picked = lax.map(one_energy, (inverses, source))
    spectrum = jnp.fft.fft(picked, axis=0) * jnp.fft.fft(screened, axis=0)
    return jnp.real(jnp.fft.ifft(spectrum, axis=0)).astype(jnp.float32)
```

```python
import functools
import math

import jax
import jax.numpy as jnp
import numpy as np
from jax import lax
from jax.experimental import pallas as pl
from jax.experimental.pallas import tpu as pltpu
from jax.sharding import PartitionSpec as P

BF = jnp.bfloat16
F32 = jnp.float32
VMEM = pl.BlockSpec(memory_space=pltpu.VMEM)
SMEM = pl.BlockSpec(memory_space=pltpu.SMEM)
ANY = pl.BlockSpec(memory_space=pl.ANY)


def params():
    return pltpu.CompilerParams(vmem_limit_bytes=48 * 1024 * 1024)


def cost(products, size=256):
    return pl.CostEstimate(flops=int(products * 3 * 2 * size**3), bytes_accessed=1 << 20, transcendentals=0)


def split(value):
    high = value.astype(BF)
    return high, (value - high.astype(F32)).astype(BF)


def product(left, right, right_dim=0):
    dims = (((1,), (right_dim,)), ((), ()))

    def one(a, b):
        return lax.dot_general(a, b, dims, preferred_element_type=F32)

    return one(left[0], right[0]) + (one(left[0], right[1]) + one(left[1], right[0]))


def sandwich(outer, inner):
    return product(split(product(outer, inner)), outer, 1)


def prepare_kernel(inv_ref, coup_ref, src_ref, map_h, map_l, add, first_h, first_l, inject):
    inv0, inv1 = split(inv_ref[0, 0]), split(inv_ref[0, 1])
    step0 = split(product(inv0, split(coup_ref[0])))
    inj0 = sandwich(inv0, split(src_ref[0, 0]))
    step1 = split(product(inv1, split(coup_ref[1])))
    inj1 = sandwich(inv1, split(src_ref[0, 1]))
    add[...] = sandwich(step1, split(inj0)) + inj1
    map_h[...], map_l[...] = split(product(step1, step0))
    first_h[...], first_l[...] = step0
    inject[...] = inj0


def prepare(inverses, coupling, source, energy):
    width = coupling.shape[1]
    square = lambda kind: jax.ShapeDtypeStruct((width, width), kind)
    block = pl.BlockSpec((1, 2, width, width), lambda i: (energy, 0, 0, 0))
    whole = pl.BlockSpec((width, width), lambda i: (0, 0))
    return pl.pallas_call(
        prepare_kernel,
        grid=(1,),
        in_specs=[block, pl.BlockSpec((2, width, width), lambda i: (0, 0, 0)), block],
        out_specs=[whole] * 6,
        out_shape=[square(BF), square(BF), square(F32), square(BF), square(BF), square(F32)],
        compiler_params=params(),
        cost_estimate=cost(9),
        name="prepare",
    )(inverses, coupling, source)


def hop_kernel(step, place, state, map_h, map_l, add, out):
    @pl.when(place[0] == step + 1)
    def _():
        out[...] = sandwich((map_h[...], map_l[...]), split(state[...])) + add[...]


def hop(step, place, state, given):
    return pl.pallas_call(
        functools.partial(hop_kernel, step),
        in_specs=[SMEM] + [VMEM] * 4,
        out_specs=VMEM,
        out_shape=jax.ShapeDtypeStruct(state.shape, F32),
        compiler_params=params(),
        cost_estimate=cost(2),
        name="hop",
    )(place, state, *given[:3])


def pick_kernel(count, place, live, rows, *refs):
    states = refs[: 2 * count]
    given = refs[2 * count : 2 * count + 12]
    out, entry, sem = refs[2 * count + 12 :]
    here = place[0]
    width = entry.shape[1]

    @pl.when(here == 0)
    def _():
        entry[...] = jnp.zeros_like(entry)

    for step in range(count):

        @pl.when(here == step + 1)
        def _():
            copies = [pltpu.make_async_copy(states[e * count + step], entry.at[e], sem.at[e]) for e in range(2)]
            for copy in copies:
                copy.start()
            for copy in copies:
                copy.wait()

    slots = rows.shape[0]
    column = lax.broadcasted_iota(jnp.int32, (slots, 2 * width), 1)
    slot = lax.broadcasted_iota(jnp.int32, (slots, 2 * width), 0)
    chosen = jnp.where((column == rows[...]) & (slot < live[0]), 1.0, 0.0).astype(BF)
    for e in range(2):
        map_h, map_l, add, first_h, first_l, inject = given[6 * e : 6 * e + 6]
        state = split(entry[e])
        last = sandwich((map_h[...], map_l[...]), state) + add[...]
        first = sandwich((first_h[...], first_l[...]), state) + inject[...]
        high, low = split(jnp.concatenate([first, last], axis=0))
        dot = lambda a, b: jnp.dot(a, b, preferred_element_type=F32)
        picked = dot(chosen, high) + dot(chosen, low)
        out[:, e] = picked.reshape(slots // 8, 8, width)


def pick(place, live, rows, states, given):
    width = given[0][2].shape[0]
    slots = rows.shape[0]
    count = len(states[0])
    return pl.pallas_call(
        functools.partial(pick_kernel, count),
        in_specs=[SMEM, SMEM, VMEM] + [ANY] * (2 * count) + [VMEM] * 12,
        out_specs=VMEM,
        out_shape=jax.ShapeDtypeStruct((slots // 8, 2, 8, width), F32),
        scratch_shapes=[pltpu.VMEM((2, width, width), F32), pltpu.SemaphoreType.DMA((2,))],
        compiler_params=params(),
        cost_estimate=cost(16),
        name="pick",
    )(place, live, rows, *states[0], *states[1], *given[0], *given[1])


def transforms(count):
    half = count // 2
    points = np.arange(count)
    waves = np.arange(half)
    angle = 2.0 * math.pi * ((waves[:, None] * points[None, :]) % count) / count
    forward = np.concatenate([np.cos(angle), -np.sin(angle)], axis=0)
    forward[half] = np.where(points % 2 == 0, 1.0, -1.0)
    weight = np.full(count, 2.0 / count)
    weight[[0, half]] = 1.0 / count
    return forward.astype(np.float32), (forward.T * weight[None, :]).astype(np.float32)


def spectrum_kernel(fwd_h, fwd_l, data, out):
    for j in range(data.shape[1]):
        out[j] = product((fwd_h[...], fwd_l[...]), split(data[:, j]))


def spectrum(matrix, data):
    count, group, width = data.shape
    return pl.pallas_call(
        spectrum_kernel,
        in_specs=[VMEM] * 3,
        out_specs=VMEM,
        out_shape=jax.ShapeDtypeStruct((group, count, width), F32),
        compiler_params=params(),
        cost_estimate=cost(2),
        name="spectrum",
    )(*matrix, data)


def convolve_kernel(fwd_h, fwd_l, inv_h, inv_l, data, other, out):
    count = data.shape[0]
    half = count // 2
    single = lax.broadcasted_iota(jnp.int32, (half, data.shape[2]), 0) == 0
    for j in range(data.shape[1]):
        left = product((fwd_h[...], fwd_l[...]), split(data[:, j]))
        right = other[j]
        real_a, imag_a = left[:half], left[half:]
        real_b, imag_b = right[:half], right[half:]
        real_p = real_a * real_b - jnp.where(single, 0.0, imag_a * imag_b)
        imag_p = jnp.where(single, imag_a * imag_b, real_a * imag_b + imag_a * real_b)
        both = jnp.concatenate([real_p, imag_p], axis=0)
        out[:, j] = product((inv_h[...], inv_l[...]), split(both))


def convolve(forward, inverse, data, other):
    count, group, width = data.shape
    return pl.pallas_call(
        convolve_kernel,
        in_specs=[VMEM] * 6,
        out_specs=VMEM,
        out_shape=jax.ShapeDtypeStruct((count, group, width), F32),
        compiler_params=params(),
        cost_estimate=cost(4),
        name="convolve",
    )(*forward, *inverse, data, other)


def exchange(chunks):
    return lax.all_to_all(chunks, "energy", split_axis=0, concat_axis=0, tiled=True)


def body(inverses, coupling, source, screened, kept_rows, live_count):
    energies, slots, width = screened.shape
    parts = lax.axis_size("energy")
    spaces = lax.axis_size("space")
    place = lax.axis_index("space").astype(jnp.int32).reshape(1)
    group = slots // parts
    count = energies * parts
    forward, inverse = [split(jnp.asarray(m)) for m in transforms(count)]

    chunks = screened.reshape(energies, parts, group, width).swapaxes(0, 1)
    other = spectrum(forward, exchange(chunks).reshape(count, group, width))

    given = [prepare(inverses, coupling, source, e) for e in range(energies)]
    outgoing = [given[e][2] for e in range(energies)]
    states = [[], []]
    for step in range(spaces - 1):
        for e in range(energies):
            state = lax.ppermute(outgoing[e], "space", [(step, step + 1)])
            states[e].append(state)
            if step + 2 < spaces:
                outgoing[e] = hop(step, place, state, given[e])

    picked = pick(place, live_count, kept_rows.reshape(slots, 1), states, given)
    data = exchange(picked).reshape(count, group, width)
    sigma = convolve(forward, inverse, data, other)
    back = exchange(sigma.reshape(parts, energies, group, width))
    return back.swapaxes(0, 1).reshape(energies, slots, width)


def solution(mesh):
    return jax.shard_map(
        body,
        mesh=mesh,
        in_specs=(
            P("energy", "space", None, None),
            P("space", None, None),
            P("energy", "space", None, None),
            P("energy", "space", None),
            P("space"),
            P("space"),
        ),
        out_specs=P("energy", "space", None),
        check_vma=False,
    )
```

```python
import functools
import math

import jax
import jax.numpy as jnp
import numpy as np
from jax import lax
from jax.experimental import pallas as pl
from jax.experimental.pallas import tpu as pltpu
from jax.sharding import PartitionSpec as P

BF = jnp.bfloat16
F32 = jnp.float32
VMEM = pl.BlockSpec(memory_space=pltpu.VMEM)
SMEM = pl.BlockSpec(memory_space=pltpu.SMEM)
HBM = pl.BlockSpec(memory_space=pltpu.HBM)


def params(mebibytes=8):
    return pltpu.CompilerParams(vmem_limit_bytes=mebibytes * 1024 * 1024)


def cost(products, size=256):
    return pl.CostEstimate(flops=int(products * 3 * 2 * size**3), bytes_accessed=1 << 20, transcendentals=0)


def split(value):
    high = value.astype(BF)
    return high, (value - high.astype(F32)).astype(BF)


def product(left, right, right_dim=0):
    dims = (((1,), (right_dim,)), ((), ()))

    def one(a, b):
        return lax.dot_general(a, b, dims, preferred_element_type=F32)

    return one(left[0], right[0]) + (one(left[0], right[1]) + one(left[1], right[0]))


def sandwich(outer, inner):
    return product(split(product(outer, inner)), outer, 1)


def prepare_kernel(energy, inv_all, coup_all, src_all, map_h, map_l, add, first_h, first_l, inject, inv, coup, src, sem):
    copies = {}
    for b in range(2):
        for n, (name, source, target) in enumerate(
            (("inv", inv_all.at[energy, b], inv), ("coup", coup_all.at[b], coup), ("src", src_all.at[energy, b], src))
        ):
            copies[name, b] = pltpu.make_async_copy(source, target.at[b], sem.at[3 * b + n])
            copies[name, b].start()
    copies["inv", 0].wait()
    copies["coup", 0].wait()
    inv0 = split(inv[0])
    step0 = split(product(inv0, split(coup[0])))
    copies["src", 0].wait()
    inj0 = sandwich(inv0, split(src[0]))
    copies["inv", 1].wait()
    copies["coup", 1].wait()
    inv1 = split(inv[1])
    step1 = split(product(inv1, split(coup[1])))
    copies["src", 1].wait()
    inj1 = sandwich(inv1, split(src[1]))
    add[...] = sandwich(step1, split(inj0)) + inj1
    map_h[...], map_l[...] = split(product(step1, step0))
    first_h[...], first_l[...] = step0
    inject[...] = inj0


def prepare(inverses, coupling, source, energy):
    width = coupling.shape[1]
    square = lambda kind: jax.ShapeDtypeStruct((width, width), kind)
    pair = pltpu.VMEM((2, width, width), F32)
    return pl.pallas_call(
        functools.partial(prepare_kernel, energy),
        in_specs=[HBM] * 3,
        out_specs=[VMEM] * 6,
        out_shape=[square(BF), square(BF), square(F32), square(BF), square(BF), square(F32)],
        scratch_shapes=[pair, pair, pair, pltpu.SemaphoreType.DMA((6,))],
        compiler_params=params(12),
        cost_estimate=cost(9),
        name="prepare",
    )(inverses, coupling, source)


def hop_kernel(step, place, state, map_h, map_l, add, out):
    @pl.when(place[0] == step + 1)
    def _():
        out[...] = sandwich((map_h[...], map_l[...]), split(state[...])) + add[...]


def hop(step, place, state, given):
    return pl.pallas_call(
        functools.partial(hop_kernel, step),
        in_specs=[SMEM] + [VMEM] * 4,
        out_specs=VMEM,
        out_shape=jax.ShapeDtypeStruct(state.shape, F32),
        compiler_params=params(),
        cost_estimate=cost(2),
        name="hop",
    )(place, state, *given[:3])


def pick_kernel(energy, count, place, live, rows, *refs):
    states = refs[:count]
    map_h, map_l, add, first_h, first_l, inject = refs[count : count + 6]
    out, entry, picked, sem = refs[-4:]
    here = place[0]
    width = entry.shape[1]

    @pl.when(here == 0)
    def _():
        entry[...] = jnp.zeros_like(entry)

    for step in range(count):

        @pl.when(here == step + 1)
        def _():
            entry[...] = states[step][...]

    slots = rows.shape[0]
    column = lax.broadcasted_iota(jnp.int32, (slots, 2 * width), 1)
    slot = lax.broadcasted_iota(jnp.int32, (slots, 2 * width), 0)
    chosen = jnp.where((column == rows[...]) & (slot < live[0]), 1.0, 0.0).astype(BF)
    state = split(entry[...])
    last = sandwich((map_h[...], map_l[...]), state) + add[...]
    first = sandwich((first_h[...], first_l[...]), state) + inject[...]
    high, low = split(jnp.concatenate([first, last], axis=0))
    dot = lambda a, b: jnp.dot(a, b, preferred_element_type=F32)
    picked[...] = (dot(chosen, high) + dot(chosen, low)).reshape(picked.shape)
    copy = pltpu.make_async_copy(picked, out.at[:, energy], sem)
    copy.start()
    copy.wait()


def pick(energy, place, live, rows, states, given, before=None):
    width = given[2].shape[0]
    slots = rows.shape[0]
    count = len(states)
    operands = [place, live, rows, *states, *given]
    specs = [SMEM, SMEM] + [VMEM] * (len(operands) - 2)
    aliases = {}
    if before is not None:
        aliases = {len(operands): 0}
        operands.append(before)
        specs.append(HBM)
    return pl.pallas_call(
        functools.partial(pick_kernel, energy, count),
        in_specs=specs,
        out_specs=HBM,
        out_shape=jax.ShapeDtypeStruct((slots // 8, 2, 8, width), F32),
        scratch_shapes=[
            pltpu.VMEM((width, width), F32),
            pltpu.VMEM((slots // 8, 8, width), F32),
            pltpu.SemaphoreType.DMA,
        ],
        input_output_aliases=aliases,
        compiler_params=params(12),
        cost_estimate=cost(8),
        name="pick",
    )(*operands)


def transforms(count):
    half = count // 2
    points = np.arange(count)
    waves = np.arange(half)
    angle = 2.0 * math.pi * ((waves[:, None] * points[None, :]) % count) / count
    forward = np.concatenate([np.cos(angle), -np.sin(angle)], axis=0)
    forward[half] = np.where(points % 2 == 0, 1.0, -1.0)
    weight = np.full(count, 2.0 / count)
    weight[[0, half]] = 1.0 / count
    return forward.astype(np.float32), (forward.T * weight[None, :]).astype(np.float32)


def stacked(matrix):
    high, low = split(jnp.asarray(matrix))
    return jnp.concatenate(
        [jnp.concatenate([high, high], axis=1), jnp.concatenate([low, jnp.zeros_like(low)], axis=1)], axis=0
    )


def apply(matrix, data):
    both = jnp.dot(matrix, jnp.concatenate(split(data), axis=0), preferred_element_type=F32)
    return both[: data.shape[0]] + both[data.shape[0] :]


def spectrum_kernel(fwd, data, out):
    for j in range(data.shape[1]):
        out[j] = apply(fwd[...], data[:, j])


def spectrum(forward, data):
    count, group, width = data.shape
    return pl.pallas_call(
        spectrum_kernel,
        in_specs=[VMEM] * 2,
        out_specs=VMEM,
        out_shape=jax.ShapeDtypeStruct((group, count, width), F32),
        compiler_params=params(),
        cost_estimate=cost(2),
        name="spectrum",
    )(forward, data)


def convolve_kernel(fwd, inv, data, other, out):
    count = data.shape[0]
    half = count // 2
    single = lax.broadcasted_iota(jnp.int32, (half, data.shape[2]), 0) == 0
    for j in range(data.shape[1]):
        left = apply(fwd[...], data[:, j])
        right = other[j]
        real_a, imag_a = left[:half], left[half:]
        real_b, imag_b = right[:half], right[half:]
        real_p = real_a * real_b - jnp.where(single, 0.0, imag_a * imag_b)
        imag_p = jnp.where(single, imag_a * imag_b, real_a * imag_b + imag_a * real_b)
        out[:, j] = apply(inv[...], jnp.concatenate([real_p, imag_p], axis=0))


def convolve(forward, inverse, data, other):
    count, group, width = data.shape
    return pl.pallas_call(
        convolve_kernel,
        in_specs=[VMEM] * 4,
        out_specs=VMEM,
        out_shape=jax.ShapeDtypeStruct((count, group, width), F32),
        compiler_params=params(),
        cost_estimate=cost(4),
        name="convolve",
    )(forward, inverse, data, other)


def exchange(chunks):
    return lax.all_to_all(chunks, "energy", split_axis=0, concat_axis=0, tiled=True)


def body(inverses, coupling, source, screened, kept_rows, live_count):
    energies, slots, width = screened.shape
    parts = lax.axis_size("energy")
    spaces = lax.axis_size("space")
    place = lax.axis_index("space").astype(jnp.int32).reshape(1)
    group = slots // parts
    count = energies * parts
    forward, inverse = [stacked(m) for m in transforms(count)]
    chunks = screened.reshape(energies, parts, group, width).swapaxes(0, 1)

    given = [prepare(inverses, coupling, source, e) for e in range(energies)]
    outgoing = [given[e][2] for e in range(energies)]
    states = [[], []]
    for step in range(spaces - 1):
        for e in range(energies):
            state = lax.ppermute(outgoing[e], "space", [(step, step + 1)])
            states[e].append(state)
            if step + 2 < spaces:
                outgoing[e] = hop(step, place, state, given[e])
        if step == 0:
            chunks = lax.optimization_barrier((chunks, *outgoing))[0]
            other = spectrum(forward, exchange(chunks).reshape(count, group, width))

    rows = kept_rows.reshape(slots, 1)
    picked = None
    for e in range(energies):
        picked = pick(e, place, live_count, rows, states[e], given[e], picked)
    data = exchange(picked).reshape(count, group, width)
    sigma = convolve(forward, inverse, data, other)
    back = exchange(sigma.reshape(parts, energies, group, width))
    return back.swapaxes(0, 1).reshape(energies, slots, width)


def solution(mesh):
    return jax.shard_map(
        body,
        mesh=mesh,
        in_specs=(
            P("energy", "space", None, None),
            P("space", None, None),
            P("energy", "space", None, None),
            P("energy", "space", None),
            P("space"),
            P("space"),
        ),
        out_specs=P("energy", "space", None),
        check_vma=False,
    )
```

```python
import functools
import math

import jax
import jax.numpy as jnp
import numpy as np
from jax import lax
from jax.experimental import pallas as pl
from jax.experimental.pallas import tpu as pltpu
from jax.sharding import PartitionSpec as P

BF = jnp.bfloat16
F32 = jnp.float32
VMEM = pl.BlockSpec(memory_space=pltpu.VMEM)
SMEM = pl.BlockSpec(memory_space=pltpu.SMEM)
HBM = pl.BlockSpec(memory_space=pltpu.HBM)


def far(array):
    return pltpu.with_memory_space_constraint(array, pltpu.HBM)


def near(array):
    return pltpu.with_memory_space_constraint(array, pltpu.VMEM)


def params(mebibytes=8):
    return pltpu.CompilerParams(vmem_limit_bytes=mebibytes * 1024 * 1024)


def cost(products, size=256):
    return pl.CostEstimate(flops=int(products * 3 * 2 * size**3), bytes_accessed=1 << 20, transcendentals=0)


def split(value):
    high = value.astype(BF)
    return high, (value - high.astype(F32)).astype(BF)


def product(left, right, right_dim=0):
    dims = (((1,), (right_dim,)), ((), ()))

    def one(a, b):
        return lax.dot_general(a, b, dims, preferred_element_type=F32)

    return one(left[0], right[0]) + (one(left[0], right[1]) + one(left[1], right[0]))


def sandwich(outer, inner):
    return product(split(product(outer, inner)), outer, 1)


def prepare_kernel(inv_all, coup_all, src_all, *refs):
    energies = inv_all.shape[0]
    outs = [refs[5 * e : 5 * e + 5] for e in range(energies)]
    inv, coup, src, kept, sem, out_sem = refs[5 * energies :]
    copies = {}

    def fetch(name, source, target):
        copies[name] = pltpu.make_async_copy(source, target, sem.at[len(copies)])
        copies[name].start()

    for e in range(energies):
        for b in range(2):
            if e == 0:
                fetch(("coup", b), coup_all.at[b], coup.at[b])
            fetch(("inv", e, b), inv_all.at[e, b], inv.at[e, b])
            fetch(("src", e, b), src_all.at[e, b], src.at[e, b])

    def ready(ref, *name):
        if name in copies:
            copies.pop(name).wait()
        return split(ref[name[1:]])

    stores = []
    for e in range(energies):
        map_h, map_l, add, first, pair = outs[e]
        step, inj = [], []
        for b in range(2):
            left = ready(inv, "inv", e, b)
            moved = product(left, ready(coup, "coup", b))
            step.append(split(moved))
            inj.append(sandwich(left, ready(src, "src", e, b)))
            if b == 0:
                kept[e, 0, 0] = moved
                kept[e, 0, 1] = inj[0]
                stores.append(pltpu.make_async_copy(kept.at[e, 0], first, out_sem.at[e, 0]))
                stores[-1].start()
        added = sandwich(step[1], split(inj[0])) + inj[1]
        mapped = product(step[1], step[0])
        add[...] = added
        map_h[...], map_l[...] = split(mapped)
        kept[e, 1, 0] = mapped
        kept[e, 1, 1] = added
        stores.append(pltpu.make_async_copy(kept.at[e, 1], pair, out_sem.at[e, 1]))
        stores[-1].start()
    for store in stores:
        store.wait()


def prepare(inverses, coupling, source):
    energies, _, width, _ = inverses.shape
    square = (width, width)
    outs = [pltpu.VMEM(square, BF)] * 2 + [pltpu.VMEM(square, F32)] + [pltpu.HBM((2, *square), F32)] * 2
    results = pl.pallas_call(
        prepare_kernel,
        in_specs=[HBM] * 3,
        out_specs=([VMEM] * 3 + [HBM] * 2) * energies,
        out_shape=outs * energies,
        scratch_shapes=[
            pltpu.VMEM(inverses.shape, F32),
            pltpu.VMEM(coupling.shape, F32),
            pltpu.VMEM(source.shape, F32),
            pltpu.VMEM((energies, 2, 2, *square), F32),
            pltpu.SemaphoreType.DMA((2 + 4 * energies,)),
            pltpu.SemaphoreType.DMA((energies, 2)),
        ],
        compiler_params=params(16),
        cost_estimate=cost(18),
        name="prepare",
    )(*[far(a) for a in (inverses, coupling, source)])
    return [results[5 * e : 5 * e + 5] for e in range(energies)]


def through(pair, state):
    return sandwich(split(pair[0]), split(state)) + pair[1]


def hop_kernel(target, skips, place, entry, before, state, map_h, map_l, add, *refs):
    out, entry_out = refs[-2:]
    active = place[0] == target

    @pl.when(active)
    def _():
        begin = through(refs[0], state[...]) if skips else state[...]
        entry_out[...] = begin
        out[...] = sandwich((map_h[...], map_l[...]), split(begin)) + add[...]

    @pl.when(jnp.logical_not(active))
    def _():
        entry_out[...] = entry[...]
        out[...] = before[...]


def hop(target, place, entry, before, state, given, pair=None, weight=2):
    operands = [place, entry, before, state, *given[:3]]
    if pair is not None:
        operands.append(pair)
    return pl.pallas_call(
        functools.partial(hop_kernel, target, pair is not None),
        in_specs=[SMEM] + [VMEM] * (len(operands) - 1),
        out_specs=[VMEM] * 2,
        out_shape=[pltpu.VMEM(state.shape, F32)] * 2,
        compiler_params=params(),
        cost_estimate=cost(weight),
        name="hop",
    )(*operands)


def pick_kernel(energy, end, late, place, live, rows, entry, state, side, map_h, map_l, add, pair, first, *refs):
    out, begin, block, picked, sem = refs[-5:]
    here = place[0]
    sideways = functools.reduce(jnp.logical_or, [here == z for z in late])
    fetch = pltpu.make_async_copy(first, block, sem.at[0])
    fetch.start()

    @pl.when(here == end)
    def _():
        begin[...] = through(pair, state[...])

    @pl.when(sideways)
    def _():
        begin[...] = side[...]

    @pl.when(jnp.logical_not(jnp.logical_or(here == end, sideways)))
    def _():
        begin[...] = entry[...]

    width = entry.shape[1]
    slots = rows.shape[0]
    column = lax.broadcasted_iota(jnp.int32, (slots, 2 * width), 1)
    slot = lax.broadcasted_iota(jnp.int32, (slots, 2 * width), 0)
    chosen = jnp.where((column == rows[...]) & (slot < live[0]), 1.0, 0.0).astype(BF)
    start = split(begin[...])
    last = sandwich((map_h[...], map_l[...]), start) + add[...]
    fetch.wait()
    high, low = split(jnp.concatenate([through(block, begin[...]), last], axis=0))
    dot = lambda a, b: jnp.dot(a, b, preferred_element_type=F32)
    picked[...] = (dot(chosen, high) + dot(chosen, low)).reshape(picked.shape)
    store = pltpu.make_async_copy(picked, out.at[:, energy], sem.at[1])
    store.start()
    store.wait()


def pick(energy, end, late, place, live, rows, entry, state, side, pair, given, before=None):
    width = entry.shape[1]
    slots = rows.shape[0]
    operands = [place, live, rows, *[near(a) for a in (entry, state, side, *given[:3])], pair, far(given[3])]
    specs = [SMEM, SMEM] + [VMEM] * (len(operands) - 3) + [HBM]
    aliases = {}
    if before is not None:
        aliases = {len(operands): 0}
        operands.append(before)
        specs.append(HBM)
    return pl.pallas_call(
        functools.partial(pick_kernel, energy, end, late),
        in_specs=specs,
        out_specs=HBM,
        out_shape=pltpu.HBM((slots // 8, 2, 8, width), F32),
        scratch_shapes=[
            pltpu.VMEM((width, width), F32),
            pltpu.VMEM((2, width, width), F32),
            pltpu.VMEM((slots // 8, 8, width), F32),
            pltpu.SemaphoreType.DMA((2,)),
        ],
        input_output_aliases=aliases,
        compiler_params=params(12),
        cost_estimate=cost(8),
        name="pick",
    )(*operands)


def transforms(count):
    half = count // 2
    points = np.arange(count)
    waves = np.arange(half)
    angle = 2.0 * math.pi * ((waves[:, None] * points[None, :]) % count) / count
    forward = np.concatenate([np.cos(angle), -np.sin(angle)], axis=0)
    forward[half] = np.where(points % 2 == 0, 1.0, -1.0)
    weight = np.full(count, 2.0 / count)
    weight[[0, half]] = 1.0 / count
    return forward.astype(np.float32), (forward.T * weight[None, :]).astype(np.float32)


def spectrum_kernel(fwd_h, fwd_l, data, out):
    for j in range(data.shape[1]):
        out[j] = product((fwd_h[...], fwd_l[...]), split(data[:, j]))


def spectrum(forward, data):
    count, group, width = data.shape
    return pl.pallas_call(
        spectrum_kernel,
        in_specs=[VMEM] * 3,
        out_specs=VMEM,
        out_shape=pltpu.VMEM((group, count, width), F32),
        compiler_params=params(),
        cost_estimate=cost(2),
        name="spectrum",
    )(*forward, far(data))


def convolve_kernel(fwd_h, fwd_l, inv_h, inv_l, data, other, out):
    count = data.shape[0]
    half = count // 2
    single = lax.broadcasted_iota(jnp.int32, (half, data.shape[2]), 0) == 0
    for j in range(data.shape[1]):
        left = product((fwd_h[...], fwd_l[...]), split(data[:, j]))
        right = other[j]
        real_a, imag_a = left[:half], left[half:]
        real_b, imag_b = right[:half], right[half:]
        real_p = real_a * real_b - jnp.where(single, 0.0, imag_a * imag_b)
        imag_p = jnp.where(single, imag_a * imag_b, real_a * imag_b + imag_a * real_b)
        out[:, j] = product((inv_h[...], inv_l[...]), split(jnp.concatenate([real_p, imag_p], axis=0)))


def convolve(forward, inverse, data, other):
    count, group, width = data.shape
    return pl.pallas_call(
        convolve_kernel,
        in_specs=[VMEM] * 6,
        out_specs=VMEM,
        out_shape=jax.ShapeDtypeStruct((count, group, width), F32),
        compiler_params=params(),
        cost_estimate=cost(4),
        name="convolve",
    )(*forward, *inverse, data, near(other))


def arrange_kernel(data, after, out, sem):
    del after
    copies = [pltpu.make_async_copy(data.at[e], out.at[:, e], sem.at[e]) for e in range(data.shape[0])]
    for copy in copies:
        copy.start()
    for copy in copies:
        copy.wait()


def arrange(data, after):
    energies, parts = data.shape[:2]
    return pl.pallas_call(
        arrange_kernel,
        in_specs=[VMEM, VMEM],
        out_specs=HBM,
        out_shape=pltpu.HBM((parts, energies, *data.shape[2:]), F32),
        scratch_shapes=[pltpu.SemaphoreType.DMA((energies,))],
        compiler_params=params(),
        cost_estimate=cost(0.1),
        name="arrange",
    )(data, after)


def exchange(chunks):
    return lax.all_to_all(chunks, "energy", split_axis=0, concat_axis=0, tiled=True)


def body(inverses, coupling, source, screened, kept_rows, live_count):
    energies, slots, width = screened.shape
    parts = lax.axis_size("energy")
    spaces = lax.axis_size("space")
    place = lax.axis_index("space").astype(jnp.int32).reshape(1)
    group = slots // parts
    count = energies * parts
    forward, inverse = [split(jnp.asarray(m)) for m in transforms(count)]

    middle = spaces // 2
    direct = list(range(middle))
    odd = list(range(middle + 1, spaces, 2))
    path = direct + odd
    given = prepare(inverses, coupling, source)
    pairs = [lax.ppermute(given[e][4], "space", [(z - 1, z) for z in odd]) for e in range(energies)]
    outgoing = [given[e][2] for e in range(energies)]
    entry = [jnp.zeros((width, width), F32)] * energies
    state = [None] * energies
    for step, (here, target) in enumerate(zip(path[:-1], path[1:])):
        for e in range(energies):
            state[e] = lax.ppermute(outgoing[e], "space", [(here, target)])
            if target != path[-1]:
                pair = pairs[e] if target in odd else None
                weight = 60 if step == 1 else 2
                outgoing[e], entry[e] = hop(target, place, entry[e], outgoing[e], state[e], given[e], pair, weight)
        if step == 0:
            chunks = arrange(screened.reshape(energies, parts, group, width), outgoing[-1])
    late = [z - 1 for z in odd]
    other = spectrum(forward, exchange(chunks).reshape(count, group, width))
    side = [lax.ppermute(outgoing[e], "space", [(path[path.index(z) - 1], z - 1) for z in odd]) for e in range(energies)]

    rows = kept_rows.reshape(slots, 1)
    other, state[0] = lax.optimization_barrier((other, state[0]))
    picked = None
    for e in range(energies):
        picked = pick(
            e, path[-1], late, place, live_count, rows, entry[e], state[e], side[e], pairs[e], given[e], picked
        )
    data = exchange(picked).reshape(count, group, width)
    sigma = convolve(forward, inverse, data, other)
    back = exchange(sigma.reshape(parts, energies, group, width))
    return back.swapaxes(0, 1).reshape(energies, slots, width)


def solution(mesh):
    return jax.shard_map(
        body,
        mesh=mesh,
        in_specs=(
            P("energy", "space", None, None),
            P("space", None, None),
            P("energy", "space", None, None),
            P("energy", "space", None),
            P("space"),
            P("space"),
        ),
        out_specs=P("energy", "space", None),
        check_vma=False,
    )
```

```python
import functools
import math

import jax
import jax.numpy as jnp
import numpy as np
from jax import lax
from jax.experimental import pallas as pl
from jax.experimental.pallas import tpu as pltpu
from jax.sharding import PartitionSpec as P

BF = jnp.bfloat16
F32 = jnp.float32
VMEM = pl.BlockSpec(memory_space=pltpu.VMEM)
SMEM = pl.BlockSpec(memory_space=pltpu.SMEM)
HBM = pl.BlockSpec(memory_space=pltpu.HBM)


def far(array):
    return pltpu.with_memory_space_constraint(array, pltpu.HBM)


def near(array):
    return pltpu.with_memory_space_constraint(array, pltpu.VMEM)


def params(mebibytes=8):
    return pltpu.CompilerParams(vmem_limit_bytes=mebibytes * 1024 * 1024)


def cost(products, size=256):
    return pl.CostEstimate(flops=int(products * 3 * 2 * size**3), bytes_accessed=1 << 20, transcendentals=0)


def split(value):
    high = value.astype(BF)
    return high, (value - high.astype(F32)).astype(BF)


def product(left, right, right_dim=0):
    dims = (((1,), (right_dim,)), ((), ()))

    def one(a, b):
        return lax.dot_general(a, b, dims, preferred_element_type=F32)

    return one(left[0], right[0]) + (one(left[0], right[1]) + one(left[1], right[0]))


def sandwich(outer, inner):
    return product(split(product(outer, inner)), outer, 1)


def prepare_kernel(senders, place, inv_all, coup_all, src_all, *refs):
    energies = inv_all.shape[0]
    outs = [refs[4 * e : 4 * e + 4] for e in range(energies)]
    inv, coup, src, kept, sem, out_sem = refs[4 * energies :]
    sends = functools.reduce(jnp.logical_or, [place[0] == z for z in senders])
    copies = {}

    def fetch(name, source, target):
        copies[name] = pltpu.make_async_copy(source, target, sem.at[len(copies)])
        copies[name].start()

    for e in range(energies):
        for b in range(2):
            if e == 0:
                fetch(("coup", b), coup_all.at[b], coup.at[b])
            fetch(("inv", e, b), inv_all.at[e, b], inv.at[e, b])
            fetch(("src", e, b), src_all.at[e, b], src.at[e, b])

    def ready(ref, *name):
        if name in copies:
            copies.pop(name).wait()
        return split(ref[name[1:]])

    for e in range(energies):
        map_h, map_l, add, _ = outs[e]
        step, inj = [], []
        for b in range(2):
            left = ready(inv, "inv", e, b)
            step.append(split(product(left, ready(coup, "coup", b))))
            inj.append(sandwich(left, ready(src, "src", e, b)))
        added = sandwich(step[1], split(inj[0])) + inj[1]
        mapped = product(step[1], step[0])
        add[...] = added
        map_h[...], map_l[...] = split(mapped)
        kept[e, 0] = mapped
        kept[e, 1] = added

    @pl.when(sends)
    def _():
        stores = [pltpu.make_async_copy(kept.at[e], outs[e][3], out_sem.at[e]) for e in range(energies)]
        for store in stores:
            store.start()
        for store in stores:
            store.wait()


def prepare(inverses, coupling, source, place, senders):
    energies, _, width, _ = inverses.shape
    square = (width, width)
    outs = [pltpu.VMEM(square, BF)] * 2 + [pltpu.VMEM(square, F32), pltpu.HBM((2, *square), F32)]
    results = pl.pallas_call(
        functools.partial(prepare_kernel, senders),
        in_specs=[SMEM] + [HBM] * 3,
        out_specs=([VMEM] * 3 + [HBM]) * energies,
        out_shape=outs * energies,
        scratch_shapes=[
            pltpu.VMEM(inverses.shape, F32),
            pltpu.VMEM(coupling.shape, F32),
            pltpu.VMEM(source.shape, F32),
            pltpu.VMEM((energies, 2, *square), F32),
            pltpu.SemaphoreType.DMA((2 + 4 * energies,)),
            pltpu.SemaphoreType.DMA((energies,)),
        ],
        compiler_params=params(16),
        cost_estimate=cost(18),
        name="prepare",
    )(place, *[far(a) for a in (inverses, coupling, source)])
    return [results[4 * e : 4 * e + 4] for e in range(energies)]


def through(pair, state):
    return sandwich(split(pair[0]), split(state)) + pair[1]


def tick_kernel(after, out):
    out[...] = after[:8, :128]


def tick(after):
    parts = lax.axis_size("energy")
    small = pl.pallas_call(
        tick_kernel,
        in_specs=[VMEM],
        out_specs=VMEM,
        out_shape=pltpu.VMEM((8, 128), F32),
        compiler_params=params(),
        cost_estimate=cost(0.01),
        name="tick",
    )(after)
    return lax.ppermute(small, "energy", [(i, i ^ 1) for i in range(parts)])


def hop_kernel(target, skips, place, entry, before, state, map_h, map_l, add, *refs):
    out, entry_out = refs[-2:]
    active = place[0] == target

    @pl.when(active)
    def _():
        begin = through(refs[0], state[...]) if skips else state[...]
        entry_out[...] = begin
        out[...] = sandwich((map_h[...], map_l[...]), split(begin)) + add[...]

    @pl.when(jnp.logical_not(active))
    def _():
        entry_out[...] = entry[...]
        out[...] = before[...]


def hop(target, place, entry, before, state, given, pair=None, weight=2):
    operands = [place, entry, before, state, *given[:3]]
    if pair is not None:
        operands.append(pair)
    return pl.pallas_call(
        functools.partial(hop_kernel, target, pair is not None),
        in_specs=[SMEM] + [VMEM] * (len(operands) - 1),
        out_specs=[VMEM] * 2,
        out_shape=[pltpu.VMEM(state.shape, F32)] * 2,
        compiler_params=params(),
        cost_estimate=cost(weight),
        name="hop",
    )(*operands)


def pick_kernel(energy, end, late, place, live, rows, entry, state, side, map_h, map_l, add, pair, *refs):
    inv_all, coup_all, src_all = refs[:3]
    out, begin, blocks, picked, sem = refs[-5:]
    here = place[0]
    sideways = functools.reduce(jnp.logical_or, [here == z for z in late])
    wanted = (inv_all.at[energy, 0], coup_all.at[0], src_all.at[energy, 0])
    fetches = [pltpu.make_async_copy(source, blocks.at[i], sem.at[i]) for i, source in enumerate(wanted)]
    for fetch in fetches:
        fetch.start()

    @pl.when(here == end)
    def _():
        begin[...] = through(pair, state[...])

    @pl.when(sideways)
    def _():
        begin[...] = side[...]

    @pl.when(jnp.logical_not(jnp.logical_or(here == end, sideways)))
    def _():
        begin[...] = entry[...]

    width = entry.shape[1]
    slots = rows.shape[0]
    column = lax.broadcasted_iota(jnp.int32, (slots, 2 * width), 1)
    slot = lax.broadcasted_iota(jnp.int32, (slots, 2 * width), 0)
    chosen = jnp.where((column == rows[...]) & (slot < live[0]), 1.0, 0.0).astype(BF)
    start = split(begin[...])
    last = sandwich((map_h[...], map_l[...]), start) + add[...]
    for fetch in fetches:
        fetch.wait()
    inner = sandwich(split(blocks[1]), start) + blocks[2]
    first = sandwich(split(blocks[0]), split(inner))
    high, low = split(jnp.concatenate([first, last], axis=0))
    dot = lambda a, b: jnp.dot(a, b, preferred_element_type=F32)
    picked[...] = (dot(chosen, high) + dot(chosen, low)).reshape(picked.shape)
    store = pltpu.make_async_copy(picked, out.at[:, energy], sem.at[3])
    store.start()
    store.wait()


def pick(energy, end, late, place, live, rows, entry, state, side, pair, given, inputs, before=None):
    width = entry.shape[1]
    slots = rows.shape[0]
    operands = [place, live, rows, *[near(a) for a in (entry, state, side, *given[:3])], pair]
    specs = [SMEM, SMEM] + [VMEM] * (len(operands) - 2) + [HBM] * 3
    operands += [far(a) for a in inputs]
    aliases = {}
    if before is not None:
        aliases = {len(operands): 0}
        operands.append(before)
        specs.append(HBM)
    return pl.pallas_call(
        functools.partial(pick_kernel, energy, end, late),
        in_specs=specs,
        out_specs=HBM,
        out_shape=pltpu.HBM((slots // 8, 2, 8, width), F32),
        scratch_shapes=[
            pltpu.VMEM((width, width), F32),
            pltpu.VMEM((3, width, width), F32),
            pltpu.VMEM((slots // 8, 8, width), F32),
            pltpu.SemaphoreType.DMA((4,)),
        ],
        input_output_aliases=aliases,
        compiler_params=params(12),
        cost_estimate=cost(8),
        name="pick",
    )(*operands)


def transforms(count):
    half = count // 2
    points = np.arange(count)
    waves = np.arange(half)
    angle = 2.0 * math.pi * ((waves[:, None] * points[None, :]) % count) / count
    forward = np.concatenate([np.cos(angle), -np.sin(angle)], axis=0)
    forward[half] = np.where(points % 2 == 0, 1.0, -1.0)
    weight = np.full(count, 2.0 / count)
    weight[[0, half]] = 1.0 / count
    return forward.astype(np.float32), (forward.T * weight[None, :]).astype(np.float32)


def spectrum_kernel(fwd_h, fwd_l, data, out):
    for j in range(data.shape[1]):
        out[j] = product((fwd_h[...], fwd_l[...]), split(data[:, j]))


def spectrum(forward, data):
    count, group, width = data.shape
    return pl.pallas_call(
        spectrum_kernel,
        in_specs=[VMEM] * 3,
        out_specs=VMEM,
        out_shape=pltpu.VMEM((group, count, width), F32),
        compiler_params=params(),
        cost_estimate=cost(2),
        name="spectrum",
    )(*forward, far(data))


def convolve_kernel(fwd_h, fwd_l, inv_h, inv_l, data, other, out):
    count = data.shape[0]
    half = count // 2
    single = lax.broadcasted_iota(jnp.int32, (half, data.shape[2]), 0) == 0
    for j in range(data.shape[1]):
        left = product((fwd_h[...], fwd_l[...]), split(data[:, j]))
        right = other[j]
        real_a, imag_a = left[:half], left[half:]
        real_b, imag_b = right[:half], right[half:]
        real_p = real_a * real_b - jnp.where(single, 0.0, imag_a * imag_b)
        imag_p = jnp.where(single, imag_a * imag_b, real_a * imag_b + imag_a * real_b)
        out[:, j] = product((inv_h[...], inv_l[...]), split(jnp.concatenate([real_p, imag_p], axis=0)))


def convolve(forward, inverse, data, other):
    count, group, width = data.shape
    return pl.pallas_call(
        convolve_kernel,
        in_specs=[VMEM] * 6,
        out_specs=VMEM,
        out_shape=jax.ShapeDtypeStruct((count, group, width), F32),
        compiler_params=params(),
        cost_estimate=cost(4),
        name="convolve",
    )(*forward, *inverse, data, near(other))


def arrange_kernel(data, after, out, sem):
    del after
    copies = [pltpu.make_async_copy(data.at[e], out.at[:, e], sem.at[e]) for e in range(data.shape[0])]
    for copy in copies:
        copy.start()
    for copy in copies:
        copy.wait()


def arrange(data, after):
    energies, parts = data.shape[:2]
    return pl.pallas_call(
        arrange_kernel,
        in_specs=[VMEM, VMEM],
        out_specs=HBM,
        out_shape=pltpu.HBM((parts, energies, *data.shape[2:]), F32),
        scratch_shapes=[pltpu.SemaphoreType.DMA((energies,))],
        compiler_params=params(),
        cost_estimate=cost(0.1),
        name="arrange",
    )(data, after)


def exchange(chunks):
    return lax.all_to_all(chunks, "energy", split_axis=0, concat_axis=0, tiled=True)


def body(inverses, coupling, source, screened, kept_rows, live_count):
    energies, slots, width = screened.shape
    parts = lax.axis_size("energy")
    spaces = lax.axis_size("space")
    place = lax.axis_index("space").astype(jnp.int32).reshape(1)
    group = slots // parts
    count = energies * parts
    forward, inverse = [split(jnp.asarray(m)) for m in transforms(count)]

    middle = spaces // 2
    direct = list(range(middle))
    odd = list(range(middle + 1, spaces, 2))
    path = direct + odd
    given = prepare(inverses, coupling, source, place, [z - 1 for z in odd])
    pairs = [lax.ppermute(given[e][3], "space", [(z - 1, z) for z in odd]) for e in range(energies)]
    outgoing = [given[e][2] for e in range(energies)]
    entry = [jnp.zeros((width, width), F32)] * energies
    state = [None] * energies
    for step, (here, target) in enumerate(zip(path[:-1], path[1:])):
        for e in range(energies):
            state[e] = lax.ppermute(outgoing[e], "space", [(here, target)])
            if target != path[-1]:
                pair = pairs[e] if target in odd else None
                weight = 200 if step in (1, 2) else 2
                outgoing[e], entry[e] = hop(target, place, entry[e], outgoing[e], state[e], given[e], pair, weight)
        if step == 0:
            chunks = arrange(screened.reshape(energies, parts, group, width), tick(outgoing[-1]))
    late = [z - 1 for z in odd]
    other = spectrum(forward, exchange(chunks).reshape(count, group, width))
    side = [lax.ppermute(outgoing[e], "space", [(path[path.index(z) - 1], z - 1) for z in odd]) for e in range(energies)]

    rows = kept_rows.reshape(slots, 1)
    inputs = (inverses, coupling, source)
    picked = None
    for e in range(energies):
        picked = pick(
            e, path[-1], late, place, live_count, rows, entry[e], state[e], side[e], pairs[e], given[e], inputs, picked
        )
    data = exchange(picked).reshape(count, group, width)
    sigma = convolve(forward, inverse, data, other)
    back = exchange(sigma.reshape(parts, energies, group, width))
    return back.swapaxes(0, 1).reshape(energies, slots, width)


def solution(mesh):
    return jax.shard_map(
        body,
        mesh=mesh,
        in_specs=(
            P("energy", "space", None, None),
            P("space", None, None),
            P("energy", "space", None, None),
            P("energy", "space", None),
            P("space"),
            P("space"),
        ),
        out_specs=P("energy", "space", None),
        check_vma=False,
    )
```

```python
import functools
import math

import jax
import jax.numpy as jnp
import numpy as np
from jax import lax
from jax.experimental import pallas as pl
from jax.experimental.pallas import tpu as pltpu
from jax.sharding import PartitionSpec as P

BF = jnp.bfloat16
F32 = jnp.float32
VMEM = pl.BlockSpec(memory_space=pltpu.VMEM)
SMEM = pl.BlockSpec(memory_space=pltpu.SMEM)
HBM = pl.BlockSpec(memory_space=pltpu.HBM)


def far(array):
    return pltpu.with_memory_space_constraint(array, pltpu.HBM)


def near(array):
    return pltpu.with_memory_space_constraint(array, pltpu.VMEM)


def params(mebibytes=8):
    return pltpu.CompilerParams(vmem_limit_bytes=mebibytes * 1024 * 1024)


def cost(products, size=256):
    return pl.CostEstimate(flops=int(products * 3 * 2 * size**3), bytes_accessed=1 << 20, transcendentals=0)


def split(value):
    high = value.astype(BF)
    return high, (value - high.astype(F32)).astype(BF)


def product(left, right, right_dim=0):
    dims = (((1,), (right_dim,)), ((), ()))

    def one(a, b):
        return lax.dot_general(a, b, dims, preferred_element_type=F32)

    return one(left[0], right[0]) + (one(left[0], right[1]) + one(left[1], right[0]))


def sandwich(outer, inner):
    return product(split(product(outer, inner)), outer, 1)


def prepare_kernel(senders, place, inv_all, coup_all, src_all, *refs):
    energies = inv_all.shape[0]
    outs = [refs[4 * e : 4 * e + 4] for e in range(energies)]
    inv, coup, src, kept, sem, out_sem = refs[4 * energies :]
    sends = functools.reduce(jnp.logical_or, [place[0] == z for z in senders])
    copies = {}

    def fetch(name, source, target):
        copies[name] = pltpu.make_async_copy(source, target, sem.at[count[0]])
        copies[name].start()
        count[0] += 1

    def fetch_block(e, b):
        if e == 0:
            fetch(("coup", b), coup_all.at[b], coup.at[b])
        fetch(("inv", e, b), inv_all.at[e, b], inv.at[e, b])
        fetch(("src", e, b), src_all.at[e, b], src.at[e, b])

    count = [0]
    order = [(e, b) for e in range(energies) for b in range(2)]
    fetch_block(*order.pop(0))

    def ready(ref, *name):
        if name in copies:
            copies.pop(name).wait()
        return split(ref[name[1:]])

    for e in range(energies):
        map_h, map_l, add, _ = outs[e]
        step, inj = [], []
        for b in range(2):
            left = ready(inv, "inv", e, b)
            right = ready(coup, "coup", b)
            middle = ready(src, "src", e, b)
            if order:
                fetch_block(*order.pop(0))
            step.append(split(product(left, right)))
            inj.append(sandwich(left, middle))
        added = sandwich(step[1], split(inj[0])) + inj[1]
        mapped = product(step[1], step[0])
        add[...] = added
        map_h[...], map_l[...] = split(mapped)
        kept[e, 0] = mapped
        kept[e, 1] = added

    @pl.when(sends)
    def _():
        stores = [pltpu.make_async_copy(kept.at[e], outs[e][3], out_sem.at[e]) for e in range(energies)]
        for store in stores:
            store.start()
        for store in stores:
            store.wait()


def prepare(inverses, coupling, source, place, senders):
    energies, _, width, _ = inverses.shape
    square = (width, width)
    outs = [pltpu.VMEM(square, BF)] * 2 + [pltpu.VMEM(square, F32), pltpu.HBM((2, *square), F32)]
    results = pl.pallas_call(
        functools.partial(prepare_kernel, senders),
        in_specs=[SMEM] + [HBM] * 3,
        out_specs=([VMEM] * 3 + [HBM]) * energies,
        out_shape=outs * energies,
        scratch_shapes=[
            pltpu.VMEM(inverses.shape, F32),
            pltpu.VMEM(coupling.shape, F32),
            pltpu.VMEM(source.shape, F32),
            pltpu.VMEM((energies, 2, *square), F32),
            pltpu.SemaphoreType.DMA((2 + 4 * energies,)),
            pltpu.SemaphoreType.DMA((energies,)),
        ],
        compiler_params=params(16),
        cost_estimate=cost(18),
        name="prepare",
    )(place, *[far(a) for a in (inverses, coupling, source)])
    return [results[4 * e : 4 * e + 4] for e in range(energies)]


def through(pair, state):
    return sandwich(split(pair[0]), split(state)) + pair[1]


def tick_kernel(after, out):
    out[...] = after[:8, :128]


def tick(after):
    parts = lax.axis_size("energy")
    small = pl.pallas_call(
        tick_kernel,
        in_specs=[VMEM],
        out_specs=VMEM,
        out_shape=pltpu.VMEM((8, 128), F32),
        compiler_params=params(),
        cost_estimate=cost(0.01),
        name="tick",
    )(after)
    return lax.ppermute(small, "energy", [(i, i ^ 1) for i in range(parts)])


def hop_kernel(target, skips, place, entry, before, state, map_h, map_l, add, *refs):
    out, entry_out = refs[-2:]
    active = place[0] == target

    @pl.when(active)
    def _():
        begin = through(refs[0], state[...]) if skips else state[...]
        entry_out[...] = begin
        out[...] = sandwich((map_h[...], map_l[...]), split(begin)) + add[...]

    @pl.when(jnp.logical_not(active))
    def _():
        entry_out[...] = entry[...]
        out[...] = before[...]


def hop(target, place, entry, before, state, given, pair=None, weight=2):
    operands = [place, entry, before, state, *given[:3]]
    if pair is not None:
        operands.append(pair)
    return pl.pallas_call(
        functools.partial(hop_kernel, target, pair is not None),
        in_specs=[SMEM] + [VMEM] * (len(operands) - 1),
        out_specs=[VMEM] * 2,
        out_shape=[pltpu.VMEM(state.shape, F32)] * 2,
        compiler_params=params(),
        cost_estimate=cost(weight),
        name="hop",
    )(*operands)


def pick_kernel(energy, end, late, place, live, rows, entry, state, side, map_h, map_l, add, pair, *refs):
    inv_all, coup_all, src_all = refs[:3]
    out, begin, blocks, picked, sem = refs[-5:]
    here = place[0]
    sideways = functools.reduce(jnp.logical_or, [here == z for z in late])
    wanted = (inv_all.at[energy, 0], coup_all.at[0], src_all.at[energy, 0])
    fetches = [pltpu.make_async_copy(source, blocks.at[i], sem.at[i]) for i, source in enumerate(wanted)]
    for fetch in fetches:
        fetch.start()

    @pl.when(here == end)
    def _():
        begin[...] = through(pair, state[...])

    @pl.when(sideways)
    def _():
        begin[...] = side[...]

    @pl.when(jnp.logical_not(jnp.logical_or(here == end, sideways)))
    def _():
        begin[...] = entry[...]

    width = entry.shape[1]
    slots = rows.shape[0]
    column = lax.broadcasted_iota(jnp.int32, (slots, 2 * width), 1)
    slot = lax.broadcasted_iota(jnp.int32, (slots, 2 * width), 0)
    chosen = jnp.where((column == rows[...]) & (slot < live[0]), 1.0, 0.0).astype(BF)
    start = split(begin[...])
    last = sandwich((map_h[...], map_l[...]), start) + add[...]
    for fetch in fetches:
        fetch.wait()
    inner = sandwich(split(blocks[1]), start) + blocks[2]
    first = sandwich(split(blocks[0]), split(inner))
    high, low = split(jnp.concatenate([first, last], axis=0))
    dot = lambda a, b: jnp.dot(a, b, preferred_element_type=F32)
    picked[...] = (dot(chosen, high) + dot(chosen, low)).reshape(picked.shape)
    store = pltpu.make_async_copy(picked, out.at[:, energy], sem.at[3])
    store.start()
    store.wait()


def pick(energy, end, late, place, live, rows, entry, state, side, pair, given, inputs, before=None):
    width = entry.shape[1]
    slots = rows.shape[0]
    operands = [place, live, rows, *[near(a) for a in (entry, state, side, *given[:3])], pair]
    specs = [SMEM, SMEM] + [VMEM] * (len(operands) - 2) + [HBM] * 3
    operands += [far(a) for a in inputs]
    aliases = {}
    if before is not None:
        aliases = {len(operands): 0}
        operands.append(before)
        specs.append(HBM)
    return pl.pallas_call(
        functools.partial(pick_kernel, energy, end, late),
        in_specs=specs,
        out_specs=HBM,
        out_shape=pltpu.HBM((slots // 8, 2, 8, width), F32),
        scratch_shapes=[
            pltpu.VMEM((width, width), F32),
            pltpu.VMEM((3, width, width), F32),
            pltpu.VMEM((slots // 8, 8, width), F32),
            pltpu.SemaphoreType.DMA((4,)),
        ],
        input_output_aliases=aliases,
        compiler_params=params(12),
        cost_estimate=cost(8),
        name="pick",
    )(*operands)


def transforms(count):
    half = count // 2
    points = np.arange(count)
    waves = np.arange(half)
    angle = 2.0 * math.pi * ((waves[:, None] * points[None, :]) % count) / count
    forward = np.concatenate([np.cos(angle), -np.sin(angle)], axis=0)
    forward[half] = np.where(points % 2 == 0, 1.0, -1.0)
    weight = np.full(count, 2.0 / count)
    weight[[0, half]] = 1.0 / count
    return forward.astype(np.float32), (forward.T * weight[None, :]).astype(np.float32)


def spectrum_kernel(fwd_h, fwd_l, data, out):
    for j in range(data.shape[1]):
        out[j] = product((fwd_h[...], fwd_l[...]), split(data[:, j]))


def spectrum(forward, data):
    count, group, width = data.shape
    return pl.pallas_call(
        spectrum_kernel,
        in_specs=[VMEM] * 3,
        out_specs=VMEM,
        out_shape=pltpu.VMEM((group, count, width), F32),
        compiler_params=params(),
        cost_estimate=cost(2),
        name="spectrum",
    )(*forward, far(data))


def convolve_kernel(fwd_h, fwd_l, inv_h, inv_l, data, other, out):
    count = data.shape[0]
    half = count // 2
    single = lax.broadcasted_iota(jnp.int32, (half, data.shape[2]), 0) == 0
    for j in range(data.shape[1]):
        left = product((fwd_h[...], fwd_l[...]), split(data[:, j]))
        right = other[j]
        real_a, imag_a = left[:half], left[half:]
        real_b, imag_b = right[:half], right[half:]
        real_p = real_a * real_b - jnp.where(single, 0.0, imag_a * imag_b)
        imag_p = jnp.where(single, imag_a * imag_b, real_a * imag_b + imag_a * real_b)
        out[:, j] = product((inv_h[...], inv_l[...]), split(jnp.concatenate([real_p, imag_p], axis=0)))


def convolve(forward, inverse, data, other):
    count, group, width = data.shape
    return pl.pallas_call(
        convolve_kernel,
        in_specs=[VMEM] * 6,
        out_specs=VMEM,
        out_shape=jax.ShapeDtypeStruct((count, group, width), F32),
        compiler_params=params(),
        cost_estimate=cost(4),
        name="convolve",
    )(*forward, *inverse, data, near(other))


def arrange_kernel(data, after, out, sem):
    del after
    copies = [pltpu.make_async_copy(data.at[e], out.at[:, e], sem.at[e]) for e in range(data.shape[0])]
    for copy in copies:
        copy.start()
    for copy in copies:
        copy.wait()


def arrange(data, after):
    energies, parts = data.shape[:2]
    return pl.pallas_call(
        arrange_kernel,
        in_specs=[VMEM, VMEM],
        out_specs=HBM,
        out_shape=pltpu.HBM((parts, energies, *data.shape[2:]), F32),
        scratch_shapes=[pltpu.SemaphoreType.DMA((energies,))],
        compiler_params=params(),
        cost_estimate=cost(0.1),
        name="arrange",
    )(data, after)


def exchange(chunks):
    return lax.all_to_all(chunks, "energy", split_axis=0, concat_axis=0, tiled=True)


def body(inverses, coupling, source, screened, kept_rows, live_count):
    energies, slots, width = screened.shape
    parts = lax.axis_size("energy")
    spaces = lax.axis_size("space")
    place = lax.axis_index("space").astype(jnp.int32).reshape(1)
    group = slots // parts
    count = energies * parts
    forward, inverse = [split(jnp.asarray(m)) for m in transforms(count)]

    middle = spaces // 2
    direct = list(range(middle))
    odd = list(range(middle + 1, spaces, 2))
    path = direct + odd
    given = prepare(inverses, coupling, source, place, [z - 1 for z in odd])
    pairs = [lax.ppermute(given[e][3], "space", [(z - 1, z) for z in odd]) for e in range(energies)]
    outgoing = [given[e][2] for e in range(energies)]
    entry = [jnp.zeros((width, width), F32)] * energies
    state = [None] * energies
    for step, (here, target) in enumerate(zip(path[:-1], path[1:])):
        for e in range(energies):
            state[e] = lax.ppermute(outgoing[e], "space", [(here, target)])
            if target != path[-1]:
                pair = pairs[e] if target in odd else None
                weight = 200 if step in (2, 3) else 2
                outgoing[e], entry[e] = hop(target, place, entry[e], outgoing[e], state[e], given[e], pair, weight)
        if step == 1:
            chunks = arrange(screened.reshape(energies, parts, group, width), tick(outgoing[-1]))
    late = [z - 1 for z in odd]
    other = spectrum(forward, exchange(chunks).reshape(count, group, width))
    side = [lax.ppermute(outgoing[e], "space", [(path[path.index(z) - 1], z - 1) for z in odd]) for e in range(energies)]

    rows = kept_rows.reshape(slots, 1)
    inputs = (inverses, coupling, source)
    picked = None
    for e in range(energies):
        picked = pick(
            e, path[-1], late, place, live_count, rows, entry[e], state[e], side[e], pairs[e], given[e], inputs, picked
        )
    data = exchange(picked).reshape(count, group, width)
    sigma = convolve(forward, inverse, data, other)
    back = exchange(sigma.reshape(parts, energies, group, width))
    return back.swapaxes(0, 1).reshape(energies, slots, width)


def solution(mesh):
    return jax.shard_map(
        body,
        mesh=mesh,
        in_specs=(
            P("energy", "space", None, None),
            P("space", None, None),
            P("energy", "space", None, None),
            P("energy", "space", None),
            P("space"),
            P("space"),
        ),
        out_specs=P("energy", "space", None),
        check_vma=False,
    )
```

```python
import functools
import math

import jax
import jax.numpy as jnp
import numpy as np
from jax import lax
from jax.experimental import pallas as pl
from jax.experimental.pallas import tpu as pltpu
from jax.sharding import PartitionSpec as P

BF = jnp.bfloat16
F32 = jnp.float32
VMEM = pl.BlockSpec(memory_space=pltpu.VMEM)
SMEM = pl.BlockSpec(memory_space=pltpu.SMEM)
HBM = pl.BlockSpec(memory_space=pltpu.HBM)


def far(array):
    return pltpu.with_memory_space_constraint(array, pltpu.HBM)


def near(array):
    return pltpu.with_memory_space_constraint(array, pltpu.VMEM)


def params(mebibytes=8):
    return pltpu.CompilerParams(vmem_limit_bytes=mebibytes * 1024 * 1024)


def cost(products, size=256):
    return pl.CostEstimate(flops=int(products * 3 * 2 * size**3), bytes_accessed=1 << 20, transcendentals=0)


def split(value):
    high = value.astype(BF)
    return high, (value - high.astype(F32)).astype(BF)


def product(left, right, right_dim=0):
    dims = (((1,), (right_dim,)), ((), ()))

    def one(a, b):
        return lax.dot_general(a, b, dims, preferred_element_type=F32)

    return one(left[0], right[0]) + (one(left[0], right[1]) + one(left[1], right[0]))


def sandwich(outer, inner):
    return product(split(product(outer, inner)), outer, 1)


def prepare_energy(e, senders, place, inputs, outs, buffers, fetched, work, kept, sem, out_sem):
    inv_all, coup_all, src_all = inputs
    inv, coup, src = buffers
    map_h, map_l, add, pair = outs

    def fetch(b):
        copies = [(inv_all.at[e, b], inv.at[e, b]), (src_all.at[e, b], src.at[e, b])]
        if b not in fetched:
            copies.append((coup_all.at[b], coup.at[b]))
            fetched.append(b)
        started = [pltpu.make_async_copy(*ends, sem.at[e, b, n]) for n, ends in enumerate(copies)]
        for copy in started:
            copy.start()
        return started

    coming = fetch(0)
    for b in range(2):
        for copy in coming:
            copy.wait()
        coming = fetch(1) if b == 0 else []
        left = split(inv[e, b])
        work[b, 0] = product(left, split(coup[b]))
        work[b, 1] = sandwich(left, split(src[e, b]))
    last = split(work[1, 0])
    added = sandwich(last, split(work[0, 1])) + work[1, 1]
    mapped = product(last, split(work[0, 0]))
    add[...] = added
    map_h[...], map_l[...] = split(mapped)
    kept[0] = mapped
    kept[1] = added

    @pl.when(functools.reduce(jnp.logical_or, [place[0] == z for z in senders]))
    def _():
        store = pltpu.make_async_copy(kept, pair, out_sem)
        store.start()
        store.wait()


def first_terms(inputs, outs, buffers, kept, sem, out_sem):
    inv_all, coup_all, src_all = inputs
    inv, coup, src = buffers
    energies = inv_all.shape[0]
    copies = [pltpu.make_async_copy(coup_all.at[0], coup.at[0], sem.at[0, 0, 2])]
    for e in range(energies):
        copies.append(pltpu.make_async_copy(inv_all.at[e, 0], inv.at[e, 0], sem.at[e, 0, 0]))
        copies.append(pltpu.make_async_copy(src_all.at[e, 0], src.at[e, 0], sem.at[e, 0, 1]))
    for copy in copies:
        copy.start()
    for copy in copies:
        copy.wait()
    right = split(coup[0])
    stores = []
    for e in range(energies):
        left = split(inv[e, 0])
        kept[e, 0] = product(left, right)
        kept[e, 1] = sandwich(left, split(src[e, 0]))
        stores.append(pltpu.make_async_copy(kept.at[e], outs.at[e], out_sem.at[e]))
        stores[-1].start()
    for store in stores:
        store.wait()


def early_kernel(senders, place, core, *refs):
    inputs, outs, (inv, coup, src, work, kept, sem, out_sem) = refs[:3], refs[3:11], refs[11:]
    fetched = []
    buffers = (inv, coup, src)
    prepare_energy(0, senders, place, inputs, outs[:4], buffers, fetched, work, kept.at[0], sem, out_sem.at[0])

    @pl.when(core[0] == 1)
    def _():
        prepare_energy(1, senders, place, inputs, outs[4:], buffers, fetched, work, kept.at[1], sem, out_sem.at[1])


def later_kernel(senders, place, core, *refs):
    inputs, before, outs, first = refs[:3], refs[3:7], refs[7:11], refs[11]
    inv, coup, src, work, kept, sem, out_sem = refs[12:]
    buffers = (inv, coup, src)

    @pl.when(core[0] == 0)
    def _():
        prepare_energy(1, senders, place, inputs, outs, buffers, [], work, kept.at[1], sem, out_sem.at[1])

    @pl.when(core[0] == 1)
    def _():
        for source, target in zip(before[:3], outs[:3]):
            target[...] = source[...]
        first_terms(inputs, first, buffers, kept, sem, out_sem)


def rest_kernel(core, *refs):
    inputs, first = refs[:3], refs[4]
    inv, coup, src, kept, sem, out_sem = refs[5:]

    @pl.when(core[0] == 0)
    def _():
        first_terms(inputs, first, (inv, coup, src), kept, sem, out_sem)


def prepare(inverses, coupling, source, place, core, senders):
    energies, _, width, _ = inverses.shape
    square = (width, width)
    inputs = [far(a) for a in (inverses, coupling, source)]
    outs = [pltpu.VMEM(square, BF)] * 2 + [pltpu.VMEM(square, F32), pltpu.HBM((2, *square), F32)]
    specs = [VMEM] * 3 + [HBM]
    first = pltpu.HBM((energies, 2, *square), F32)
    buffers = [pltpu.VMEM(a.shape, F32) for a in (inverses, coupling, source)]
    work = pltpu.VMEM((2, 2, *square), F32)
    kept = pltpu.VMEM((energies, 2, *square), F32)
    sems = [pltpu.SemaphoreType.DMA((energies, 2, 3)), pltpu.SemaphoreType.DMA((energies,))]
    early = pl.pallas_call(
        functools.partial(early_kernel, senders),
        in_specs=[SMEM] * 2 + [HBM] * 3,
        out_specs=specs * energies,
        out_shape=outs * energies,
        scratch_shapes=buffers + [work, kept] + sems,
        compiler_params=params(16),
        cost_estimate=cost(12),
        name="prepare_early",
    )(place, core, *inputs)
    later = pl.pallas_call(
        functools.partial(later_kernel, senders),
        in_specs=[SMEM] * 2 + [HBM] * 3 + specs,
        out_specs=specs + [HBM],
        out_shape=outs + [first],
        input_output_aliases={8: 3},
        scratch_shapes=buffers + [work, kept] + sems,
        compiler_params=params(16),
        cost_estimate=cost(9),
        name="prepare_later",
    )(place, core, *inputs, *early[4:])
    first = pl.pallas_call(
        rest_kernel,
        in_specs=[SMEM] + [HBM] * 4,
        out_specs=HBM,
        out_shape=first,
        input_output_aliases={4: 0},
        scratch_shapes=buffers + [kept] + sems,
        compiler_params=params(16),
        cost_estimate=cost(4),
        name="first_terms",
    )(core, *inputs, later[4])
    return [early[:4], later[:4]], first


def through(pair, state):
    return sandwich(split(pair[0]), split(state)) + pair[1]


def tick_kernel(after, out):
    out[...] = after[:8, :128]


def tick(after):
    parts = lax.axis_size("energy")
    small = pl.pallas_call(
        tick_kernel,
        in_specs=[VMEM],
        out_specs=VMEM,
        out_shape=pltpu.VMEM((8, 128), F32),
        compiler_params=params(),
        cost_estimate=cost(0.01),
        name="tick",
    )(after)
    return lax.ppermute(small, "energy", [(i, i ^ 1) for i in range(parts)])


def hop_kernel(target, skips, place, entry, before, state, map_h, map_l, add, *refs):
    out, entry_out = refs[-2:]
    active = place[0] == target

    @pl.when(active)
    def _():
        begin = through(refs[0], state[...]) if skips else state[...]
        entry_out[...] = begin
        out[...] = sandwich((map_h[...], map_l[...]), split(begin)) + add[...]

    @pl.when(jnp.logical_not(active))
    def _():
        entry_out[...] = entry[...]
        out[...] = before[...]


def hop(target, place, entry, before, state, given, pair=None, weight=2):
    operands = [place, entry, before, state, *given[:3]]
    if pair is not None:
        operands.append(pair)
    return pl.pallas_call(
        functools.partial(hop_kernel, target, pair is not None),
        in_specs=[SMEM] + [VMEM] * (len(operands) - 1),
        out_specs=[VMEM] * 2,
        out_shape=[pltpu.VMEM(state.shape, F32)] * 2,
        compiler_params=params(),
        cost_estimate=cost(weight),
        name="hop",
    )(*operands)


def pick_kernel(energy, end, late, place, live, rows, entry, state, side, map_h, map_l, add, pair, *refs):
    first_all = refs[0]
    out, begin, block, picked, sem = refs[-5:]
    here = place[0]
    sideways = functools.reduce(jnp.logical_or, [here == z for z in late])
    fetch = pltpu.make_async_copy(first_all.at[energy], block, sem.at[0])
    fetch.start()

    @pl.when(here == end)
    def _():
        begin[...] = through(pair, state[...])

    @pl.when(sideways)
    def _():
        begin[...] = side[...]

    @pl.when(jnp.logical_not(jnp.logical_or(here == end, sideways)))
    def _():
        begin[...] = entry[...]

    width = entry.shape[1]
    slots = rows.shape[0]
    column = lax.broadcasted_iota(jnp.int32, (slots, 2 * width), 1)
    slot = lax.broadcasted_iota(jnp.int32, (slots, 2 * width), 0)
    chosen = jnp.where((column == rows[...]) & (slot < live[0]), 1.0, 0.0).astype(BF)
    start = split(begin[...])
    last = sandwich((map_h[...], map_l[...]), start) + add[...]
    fetch.wait()
    high, low = split(jnp.concatenate([sandwich(split(block[0]), start) + block[1], last], axis=0))
    dot = lambda a, b: jnp.dot(a, b, preferred_element_type=F32)
    stores = []
    half = slots // 2
    for n in range(2):
        rows_in, groups = slice(n * half, (n + 1) * half), pl.ds(n * half // 8, half // 8)
        picked[groups] = (dot(chosen[rows_in], high) + dot(chosen[rows_in], low)).reshape(half // 8, 8, width)
        stores.append(pltpu.make_async_copy(picked.at[groups], out.at[groups, energy], sem.at[1 + n]))
        stores[-1].start()
    for store in stores:
        store.wait()


def pick(energy, end, late, place, live, rows, entry, state, side, pair, given, first, before=None):
    width = entry.shape[1]
    slots = rows.shape[0]
    operands = [place, live, rows, *[near(a) for a in (entry, state, side, *given[:3])], pair]
    specs = [SMEM, SMEM] + [VMEM] * (len(operands) - 2) + [HBM]
    operands.append(far(first))
    aliases = {}
    if before is not None:
        aliases = {len(operands): 0}
        operands.append(before)
        specs.append(HBM)
    return pl.pallas_call(
        functools.partial(pick_kernel, energy, end, late),
        in_specs=specs,
        out_specs=HBM,
        out_shape=pltpu.HBM((slots // 8, 2, 8, width), F32),
        scratch_shapes=[
            pltpu.VMEM((width, width), F32),
            pltpu.VMEM((2, width, width), F32),
            pltpu.VMEM((slots // 8, 8, width), F32),
            pltpu.SemaphoreType.DMA((3,)),
        ],
        input_output_aliases=aliases,
        compiler_params=params(12),
        cost_estimate=cost(8),
        name="pick",
    )(*operands)


def transforms(count):
    half = count // 2
    points = np.arange(count)
    waves = np.arange(half)
    angle = 2.0 * math.pi * ((waves[:, None] * points[None, :]) % count) / count
    forward = np.concatenate([np.cos(angle), -np.sin(angle)], axis=0)
    forward[half] = np.where(points % 2 == 0, 1.0, -1.0)
    weight = np.full(count, 2.0 / count)
    weight[[0, half]] = 1.0 / count
    return forward.astype(np.float32), (forward.T * weight[None, :]).astype(np.float32)


def spectrum_kernel(fwd_h, fwd_l, data, out):
    for j in range(data.shape[1]):
        out[j] = product((fwd_h[...], fwd_l[...]), split(data[:, j]))


def spectrum(forward, data):
    count, group, width = data.shape
    return pl.pallas_call(
        spectrum_kernel,
        in_specs=[VMEM] * 3,
        out_specs=VMEM,
        out_shape=pltpu.VMEM((group, count, width), F32),
        compiler_params=params(),
        cost_estimate=cost(2),
        name="spectrum",
    )(*forward, far(data))


def convolve_kernel(fwd_h, fwd_l, inv_h, inv_l, data, other, out):
    count = data.shape[0]
    half = count // 2
    single = lax.broadcasted_iota(jnp.int32, (half, data.shape[2]), 0) == 0
    for j in range(data.shape[1]):
        left = product((fwd_h[...], fwd_l[...]), split(data[:, j]))
        right = other[j]
        real_a, imag_a = left[:half], left[half:]
        real_b, imag_b = right[:half], right[half:]
        real_p = real_a * real_b - jnp.where(single, 0.0, imag_a * imag_b)
        imag_p = jnp.where(single, imag_a * imag_b, real_a * imag_b + imag_a * real_b)
        out[:, j] = product((inv_h[...], inv_l[...]), split(jnp.concatenate([real_p, imag_p], axis=0)))


def convolve(forward, inverse, data, other):
    count, group, width = data.shape
    return pl.pallas_call(
        convolve_kernel,
        in_specs=[VMEM] * 6,
        out_specs=VMEM,
        out_shape=jax.ShapeDtypeStruct((count, group, width), F32),
        compiler_params=params(),
        cost_estimate=cost(4),
        name="convolve",
    )(*forward, *inverse, data, near(other))


def arrange_kernel(data, after, out, sem):
    del after
    copies = [pltpu.make_async_copy(data.at[e], out.at[:, e], sem.at[e]) for e in range(data.shape[0])]
    for copy in copies:
        copy.start()
    for copy in copies:
        copy.wait()


def arrange(data, after):
    energies, parts = data.shape[:2]
    return pl.pallas_call(
        arrange_kernel,
        in_specs=[VMEM, VMEM],
        out_specs=HBM,
        out_shape=pltpu.HBM((parts, energies, *data.shape[2:]), F32),
        scratch_shapes=[pltpu.SemaphoreType.DMA((energies,))],
        compiler_params=params(),
        cost_estimate=cost(0.1),
        name="arrange",
    )(data, after)


def exchange(chunks):
    return lax.all_to_all(chunks, "energy", split_axis=0, concat_axis=0, tiled=True)


def body(inverses, coupling, source, screened, kept_rows, live_count):
    energies, slots, width = screened.shape
    parts = lax.axis_size("energy")
    spaces = lax.axis_size("space")
    place = lax.axis_index("space").astype(jnp.int32).reshape(1)
    group = slots // parts
    count = energies * parts
    forward, inverse = [split(jnp.asarray(m)) for m in transforms(count)]

    middle = spaces // 2
    direct = list(range(middle))
    odd = list(range(middle + 1, spaces, 2))
    path = direct + odd
    core = (lax.axis_index("energy").astype(jnp.int32) % 2).reshape(1)
    given, first = prepare(inverses, coupling, source, place, core, [z - 1 for z in odd])
    pairs = [lax.ppermute(given[e][3], "space", [(z - 1, z) for z in odd]) for e in range(energies)]
    outgoing = [given[e][2] for e in range(energies)]
    entry = [jnp.zeros((width, width), F32)] * energies
    state = [None] * energies
    for step, (here, target) in enumerate(zip(path[:-1], path[1:])):
        for e in range(energies):
            state[e] = lax.ppermute(outgoing[e], "space", [(here, target)])
            if target != path[-1]:
                pair = pairs[e] if target in odd else None
                weight = 200 if step in (2, 3) else 2
                outgoing[e], entry[e] = hop(target, place, entry[e], outgoing[e], state[e], given[e], pair, weight)
        if step == 1:
            chunks = arrange(screened.reshape(energies, parts, group, width), tick(outgoing[-1]))
    late = [z - 1 for z in odd]
    other = spectrum(forward, exchange(chunks).reshape(count, group, width))
    side = [lax.ppermute(outgoing[e], "space", [(path[path.index(z) - 1], z - 1) for z in odd]) for e in range(energies)]

    rows = kept_rows.reshape(slots, 1)
    picked = None
    for e in range(energies):
        picked = pick(
            e, path[-1], late, place, live_count, rows, entry[e], state[e], side[e], pairs[e], given[e], first, picked
        )
    data = exchange(picked).reshape(count, group, width)
    sigma = convolve(forward, inverse, data, other)
    back = exchange(sigma.reshape(parts, energies, group, width))
    return back.swapaxes(0, 1).reshape(energies, slots, width)


def solution(mesh):
    return jax.shard_map(
        body,
        mesh=mesh,
        in_specs=(
            P("energy", "space", None, None),
            P("space", None, None),
            P("energy", "space", None, None),
            P("energy", "space", None),
            P("space"),
            P("space"),
        ),
        out_specs=P("energy", "space", None),
        check_vma=False,
    )
```

```python
import functools
import math

import jax
import jax.numpy as jnp
import numpy as np
from jax import lax
from jax.experimental import pallas as pl
from jax.experimental.pallas import tpu as pltpu
from jax.sharding import PartitionSpec as P

BF = jnp.bfloat16
F32 = jnp.float32
VMEM = pl.BlockSpec(memory_space=pltpu.VMEM)
SMEM = pl.BlockSpec(memory_space=pltpu.SMEM)
HBM = pl.BlockSpec(memory_space=pltpu.HBM)


def far(array):
    return pltpu.with_memory_space_constraint(array, pltpu.HBM)


def near(array):
    return pltpu.with_memory_space_constraint(array, pltpu.VMEM)


def params(mebibytes=8):
    return pltpu.CompilerParams(vmem_limit_bytes=mebibytes * 1024 * 1024)


def cost(products, size=256):
    return pl.CostEstimate(flops=int(products * 3 * 2 * size**3), bytes_accessed=1 << 20, transcendentals=0)


def split(value):
    high = value.astype(BF)
    return high, (value - high.astype(F32)).astype(BF)


def product(left, right, right_dim=0):
    dims = (((1,), (right_dim,)), ((), ()))

    def one(a, b):
        return lax.dot_general(a, b, dims, preferred_element_type=F32)

    return one(left[0], right[0]) + (one(left[0], right[1]) + one(left[1], right[0]))


def sandwich(outer, inner):
    return product(split(product(outer, inner)), outer, 1)


def prepare_kernel(senders, place, inv_all, coup_all, src_all, *refs):
    energies = inv_all.shape[0]
    outs = [refs[4 * e : 4 * e + 4] for e in range(energies)]
    inv, coup, src, kept, sem, out_sem = refs[4 * energies :]
    sends = functools.reduce(jnp.logical_or, [place[0] == z for z in senders])
    copies = {}

    def fetch(name, source, target):
        copies[name] = pltpu.make_async_copy(source, target, sem.at[count[0]])
        copies[name].start()
        count[0] += 1

    def fetch_block(e, b):
        if e == 0:
            fetch(("coup", b), coup_all.at[b], coup.at[b])
        fetch(("inv", e, b), inv_all.at[e, b], inv.at[e, b])
        fetch(("src", e, b), src_all.at[e, b], src.at[e, b])

    count = [0]
    order = [(e, b) for e in range(energies) for b in range(2)]
    fetch_block(*order.pop(0))

    def ready(ref, *name):
        if name in copies:
            copies.pop(name).wait()
        return split(ref[name[1:]])

    for e in range(energies):
        map_h, map_l, add, _ = outs[e]
        step, inj = [], []
        for b in range(2):
            left = ready(inv, "inv", e, b)
            right = ready(coup, "coup", b)
            middle = ready(src, "src", e, b)
            if order:
                fetch_block(*order.pop(0))
            step.append(split(product(left, right)))
            inj.append(sandwich(left, middle))
        added = sandwich(step[1], split(inj[0])) + inj[1]
        mapped = product(step[1], step[0])
        add[...] = added
        map_h[...], map_l[...] = split(mapped)
        kept[e, 0] = mapped
        kept[e, 1] = added

    @pl.when(sends)
    def _():
        stores = [pltpu.make_async_copy(kept.at[e], outs[e][3], out_sem.at[e]) for e in range(energies)]
        for store in stores:
            store.start()
        for store in stores:
            store.wait()


def prepare(inverses, coupling, source, place, senders):
    energies, _, width, _ = inverses.shape
    square = (width, width)
    outs = [pltpu.VMEM(square, BF)] * 2 + [pltpu.VMEM(square, F32), pltpu.HBM((2, *square), F32)]
    results = pl.pallas_call(
        functools.partial(prepare_kernel, senders),
        in_specs=[SMEM] + [HBM] * 3,
        out_specs=([VMEM] * 3 + [HBM]) * energies,
        out_shape=outs * energies,
        scratch_shapes=[
            pltpu.VMEM(inverses.shape, F32),
            pltpu.VMEM(coupling.shape, F32),
            pltpu.VMEM(source.shape, F32),
            pltpu.VMEM((energies, 2, *square), F32),
            pltpu.SemaphoreType.DMA((2 + 4 * energies,)),
            pltpu.SemaphoreType.DMA((energies,)),
        ],
        compiler_params=params(16),
        cost_estimate=cost(18),
        name="prepare",
    )(place, *[far(a) for a in (inverses, coupling, source)])
    return [results[4 * e : 4 * e + 4] for e in range(energies)]


def through(pair, state):
    return sandwich(split(pair[0]), split(state)) + pair[1]


def hop_kernel(target, skips, place, entry, before, state, map_h, map_l, add, *refs):
    out, entry_out = refs[-2:]
    active = place[0] == target

    @pl.when(active)
    def _():
        begin = through(refs[0], state[...]) if skips else state[...]
        entry_out[...] = begin
        out[...] = sandwich((map_h[...], map_l[...]), split(begin)) + add[...]

    @pl.when(jnp.logical_not(active))
    def _():
        entry_out[...] = entry[...]
        out[...] = before[...]


def hop(target, place, entry, before, state, given, pair=None, weight=2):
    operands = [place, entry, before, state, *given[:3]]
    if pair is not None:
        operands.append(pair)
    return pl.pallas_call(
        functools.partial(hop_kernel, target, pair is not None),
        in_specs=[SMEM] + [VMEM] * (len(operands) - 1),
        out_specs=[VMEM] * 2,
        out_shape=[pltpu.VMEM(state.shape, F32)] * 2,
        compiler_params=params(),
        cost_estimate=cost(weight),
        name="hop",
    )(*operands)


def first_kernel(inv_all, coup_all, src_all, out, inv, coup, src, kept, sem):
    energies = inv_all.shape[0]
    copies = [pltpu.make_async_copy(coup_all.at[0], coup, sem.at[0])]
    for e in range(energies):
        copies.append(pltpu.make_async_copy(inv_all.at[e, 0], inv.at[e], sem.at[1 + 2 * e]))
        copies.append(pltpu.make_async_copy(src_all.at[e, 0], src.at[e], sem.at[2 + 2 * e]))
    for copy in copies:
        copy.start()
    for copy in copies:
        copy.wait()
    right = split(coup[...])
    stores = []
    for e in range(energies):
        left = split(inv[e])
        kept[e, 0] = product(left, right)
        kept[e, 1] = sandwich(left, split(src[e]))
        stores.append(pltpu.make_async_copy(kept.at[e], out.at[e], sem.at[1 + 2 * energies + e]))
        stores[-1].start()
    for store in stores:
        store.wait()


def first_terms(inverses, coupling, source):
    energies, _, width, _ = inverses.shape
    square = (width, width)
    return pl.pallas_call(
        first_kernel,
        in_specs=[HBM] * 3,
        out_specs=HBM,
        out_shape=pltpu.HBM((energies, 2, *square), F32),
        scratch_shapes=[
            pltpu.VMEM((energies, *square), F32),
            pltpu.VMEM(square, F32),
            pltpu.VMEM((energies, *square), F32),
            pltpu.VMEM((energies, 2, *square), F32),
            pltpu.SemaphoreType.DMA((1 + 3 * energies,)),
        ],
        compiler_params=params(16),
        cost_estimate=cost(6),
        name="first_terms",
    )(*[far(a) for a in (inverses, coupling, source)])


def pick_kernel(energy, end, late, place, live, rows, entry, state, side, map_h, map_l, add, pair, *refs):
    first_all = refs[0]
    out, begin, block, picked, sem = refs[-5:]
    here = place[0]
    sideways = functools.reduce(jnp.logical_or, [here == z for z in late])
    fetch = pltpu.make_async_copy(first_all.at[energy], block, sem.at[0])
    fetch.start()

    @pl.when(here == end)
    def _():
        begin[...] = through(pair, state[...])

    @pl.when(sideways)
    def _():
        begin[...] = side[...]

    @pl.when(jnp.logical_not(jnp.logical_or(here == end, sideways)))
    def _():
        begin[...] = entry[...]

    width = entry.shape[1]
    slots = rows.shape[0]
    column = lax.broadcasted_iota(jnp.int32, (slots, 2 * width), 1)
    slot = lax.broadcasted_iota(jnp.int32, (slots, 2 * width), 0)
    chosen = jnp.where((column == rows[...]) & (slot < live[0]), 1.0, 0.0).astype(BF)
    start = split(begin[...])
    last = sandwich((map_h[...], map_l[...]), start) + add[...]
    fetch.wait()
    high, low = split(jnp.concatenate([sandwich(split(block[0]), start) + block[1], last], axis=0))
    dot = lambda a, b: jnp.dot(a, b, preferred_element_type=F32)
    stores = []
    half = slots // 2
    for n in range(2):
        rows_in, groups = slice(n * half, (n + 1) * half), pl.ds(n * half // 8, half // 8)
        picked[groups] = (dot(chosen[rows_in], high) + dot(chosen[rows_in], low)).reshape(half // 8, 8, width)
        stores.append(pltpu.make_async_copy(picked.at[groups], out.at[groups, energy], sem.at[1 + n]))
        stores[-1].start()
    for store in stores:
        store.wait()


def pick(energy, end, late, place, live, rows, entry, state, side, pair, given, first, before=None):
    width = entry.shape[1]
    slots = rows.shape[0]
    operands = [place, live, rows, *[near(a) for a in (entry, state, side, *given[:3])], pair]
    specs = [SMEM, SMEM] + [VMEM] * (len(operands) - 2) + [HBM]
    operands.append(far(first))
    aliases = {}
    if before is not None:
        aliases = {len(operands): 0}
        operands.append(before)
        specs.append(HBM)
    return pl.pallas_call(
        functools.partial(pick_kernel, energy, end, late),
        in_specs=specs,
        out_specs=HBM,
        out_shape=pltpu.HBM((slots // 8, 2, 8, width), F32),
        scratch_shapes=[
            pltpu.VMEM((width, width), F32),
            pltpu.VMEM((2, width, width), F32),
            pltpu.VMEM((slots // 8, 8, width), F32),
            pltpu.SemaphoreType.DMA((3,)),
        ],
        input_output_aliases=aliases,
        compiler_params=params(12),
        cost_estimate=cost(8),
        name="pick",
    )(*operands)


def transforms(count):
    half = count // 2
    points = np.arange(count)
    waves = np.arange(half)
    angle = 2.0 * math.pi * ((waves[:, None] * points[None, :]) % count) / count
    forward = np.concatenate([np.cos(angle), -np.sin(angle)], axis=0)
    forward[half] = np.where(points % 2 == 0, 1.0, -1.0)
    weight = np.full(count, 2.0 / count)
    weight[[0, half]] = 1.0 / count
    return forward.astype(np.float32), (forward.T * weight[None, :]).astype(np.float32)


def stacked(matrix):
    return jnp.concatenate(split(jnp.asarray(matrix)), axis=0)


def transform(matrix, data):
    count = data.shape[0]
    high, low = split(data)
    dot = lambda a, b: jnp.dot(a, b, preferred_element_type=F32)
    both = dot(matrix, high)
    return both[:count] + (both[count:] + dot(matrix[:count], low))


def spectrum_kernel(fwd, data, out):
    columns = jnp.swapaxes(data[...], 0, 1)
    for j in range(columns.shape[0]):
        out[j] = transform(fwd[...], columns[j])


def spectrum(forward, data):
    count, group, width = data.shape
    return pl.pallas_call(
        spectrum_kernel,
        in_specs=[VMEM] * 2,
        out_specs=VMEM,
        out_shape=pltpu.VMEM((group, count, width), F32),
        compiler_params=params(),
        cost_estimate=cost(2),
        name="spectrum",
    )(forward, far(data))


def convolve_kernel(fwd, inv, data, other, out):
    half = data.shape[0] // 2
    single = lax.broadcasted_iota(jnp.int32, (half, data.shape[2]), 0) == 0
    columns = jnp.swapaxes(data[...], 0, 1)
    results = []
    for j in range(columns.shape[0]):
        left = transform(fwd[...], columns[j])
        right = other[j]
        real_a, imag_a = left[:half], left[half:]
        real_b, imag_b = right[:half], right[half:]
        real_p = real_a * real_b - jnp.where(single, 0.0, imag_a * imag_b)
        imag_p = jnp.where(single, imag_a * imag_b, real_a * imag_b + imag_a * real_b)
        results.append(transform(inv[...], jnp.concatenate([real_p, imag_p], axis=0)))
    out[...] = jnp.swapaxes(jnp.stack(results), 0, 1)


def convolve(forward, inverse, data, other):
    count, group, width = data.shape
    return pl.pallas_call(
        convolve_kernel,
        in_specs=[VMEM] * 4,
        out_specs=VMEM,
        out_shape=jax.ShapeDtypeStruct((count, group, width), F32),
        compiler_params=params(),
        cost_estimate=cost(4),
        name="convolve",
    )(forward, inverse, data, near(other))


def arrange_kernel(data, after, out, sem):
    del after
    copies = [pltpu.make_async_copy(data.at[e], out.at[:, e], sem.at[e]) for e in range(data.shape[0])]
    for copy in copies:
        copy.start()
    for copy in copies:
        copy.wait()


def arrange(data, after):
    energies, parts = data.shape[:2]
    return pl.pallas_call(
        arrange_kernel,
        in_specs=[VMEM, VMEM],
        out_specs=HBM,
        out_shape=pltpu.HBM((parts, energies, *data.shape[2:]), F32),
        scratch_shapes=[pltpu.SemaphoreType.DMA((energies,))],
        compiler_params=params(),
        cost_estimate=cost(0.1),
        name="arrange",
    )(data, after)


def exchange(chunks):
    return lax.all_to_all(chunks, "energy", split_axis=0, concat_axis=0, tiled=True)


def body(inverses, coupling, source, screened, kept_rows, live_count):
    energies, slots, width = screened.shape
    parts = lax.axis_size("energy")
    spaces = lax.axis_size("space")
    place = lax.axis_index("space").astype(jnp.int32).reshape(1)
    group = slots // parts
    count = energies * parts
    forward, inverse = [stacked(m) for m in transforms(count)]

    middle = spaces // 2
    direct = list(range(middle))
    odd = list(range(middle + 1, spaces, 2))
    path = direct + odd
    given = prepare(inverses, coupling, source, place, [z - 1 for z in odd])
    pairs = [lax.ppermute(given[e][3], "space", [(z - 1, z) for z in odd]) for e in range(energies)]
    outgoing = [given[e][2] for e in range(energies)]
    entry = [jnp.zeros((width, width), F32)] * energies
    state = [None] * energies
    for step, (here, target) in enumerate(zip(path[:-1], path[1:])):
        for e in range(energies):
            state[e] = lax.ppermute(outgoing[e], "space", [(here, target)])
            if target != path[-1]:
                pair = pairs[e] if target in odd else None
                weight = 200 if step in (2, 3) else 2
                outgoing[e], entry[e] = hop(target, place, entry[e], outgoing[e], state[e], given[e], pair, weight)
        if step == 1:
            chunks = arrange(screened.reshape(energies, parts, group, width), outgoing[-1])
    late = [z - 1 for z in odd]
    other = spectrum(forward, exchange(chunks).reshape(count, group, width))
    side = [lax.ppermute(outgoing[e], "space", [(path[path.index(z) - 1], z - 1) for z in odd]) for e in range(energies)]

    rows = kept_rows.reshape(slots, 1)
    first = first_terms(inverses, coupling, source)
    picked = None
    for e in range(energies):
        picked = pick(
            e, path[-1], late, place, live_count, rows, entry[e], state[e], side[e], pairs[e], given[e], first, picked
        )
    data = exchange(picked).reshape(count, group, width)
    sigma = convolve(forward, inverse, data, other)
    back = exchange(sigma.reshape(parts, energies, group, width))
    return back.swapaxes(0, 1).reshape(energies, slots, width)


def solution(mesh):
    return jax.shard_map(
        body,
        mesh=mesh,
        in_specs=(
            P("energy", "space", None, None),
            P("space", None, None),
            P("energy", "space", None, None),
            P("energy", "space", None),
            P("space"),
            P("space"),
        ),
        out_specs=P("energy", "space", None),
        check_vma=False,
    )
```

```python
import functools
import math

import jax
import jax.numpy as jnp
import numpy as np
from jax import lax
from jax.experimental import pallas as pl
from jax.experimental.pallas import tpu as pltpu
from jax.sharding import PartitionSpec as P

BF = jnp.bfloat16
F32 = jnp.float32
VMEM = pl.BlockSpec(memory_space=pltpu.VMEM)
SMEM = pl.BlockSpec(memory_space=pltpu.SMEM)
HBM = pl.BlockSpec(memory_space=pltpu.HBM)


def far(array):
    return pltpu.with_memory_space_constraint(array, pltpu.HBM)


def near(array):
    return pltpu.with_memory_space_constraint(array, pltpu.VMEM)


def params(mebibytes=8):
    return pltpu.CompilerParams(vmem_limit_bytes=mebibytes * 1024 * 1024)


def cost(products, size=256):
    return pl.CostEstimate(flops=int(products * 3 * 2 * size**3), bytes_accessed=1 << 20, transcendentals=0)


def split(value):
    high = value.astype(BF)
    return high, (value - high.astype(F32)).astype(BF)


def product(left, right, right_dim=0):
    dims = (((1,), (right_dim,)), ((), ()))

    def one(a, b):
        return lax.dot_general(a, b, dims, preferred_element_type=F32)

    return one(left[0], right[0]) + (one(left[0], right[1]) + one(left[1], right[0]))


def sandwich(outer, inner):
    return product(split(product(outer, inner)), outer, 1)


def prepare_kernel(senders, place, inv_all, coup_all, src_all, *refs):
    energies = inv_all.shape[0]
    outs = [refs[4 * e : 4 * e + 4] for e in range(energies)]
    inv, coup, src, work, kept, sem, out_sem = refs[4 * energies :]
    sends = functools.reduce(jnp.logical_or, [place[0] == z for z in senders])
    copies = {}

    def fetch(name, source, target):
        copies[name] = pltpu.make_async_copy(source, target, sem.at[count[0]])
        copies[name].start()
        count[0] += 1

    def fetch_block(e, b):
        if e == 0:
            fetch(("coup", b), coup_all.at[b], coup.at[b])
        fetch(("inv", e, b), inv_all.at[e, b], inv.at[e, b])
        fetch(("src", e, b), src_all.at[e, b], src.at[e, b])

    count = [0]
    order = [(e, b) for e in range(energies) for b in range(2)]
    fetch_block(*order.pop(0))

    def ready(ref, *name):
        if name in copies:
            copies.pop(name).wait()
        return split(ref[name[1:]])

    for e in range(energies):
        map_h, map_l, add, _ = outs[e]
        for b in range(2):
            left = ready(inv, "inv", e, b)
            right = ready(coup, "coup", b)
            middle = ready(src, "src", e, b)
            if order:
                fetch_block(*order.pop(0))
            work[e, b, 0] = product(left, right)
            work[e, b, 1] = sandwich(left, middle)
        last = split(work[e, 1, 0])
        added = sandwich(last, split(work[e, 0, 1])) + work[e, 1, 1]
        mapped = product(last, split(work[e, 0, 0]))
        add[...] = added
        map_h[...], map_l[...] = split(mapped)
        kept[e, 0] = mapped
        kept[e, 1] = added

    @pl.when(sends)
    def _():
        stores = [pltpu.make_async_copy(kept.at[e], outs[e][3], out_sem.at[e]) for e in range(energies)]
        for store in stores:
            store.start()
        for store in stores:
            store.wait()


def prepare(inverses, coupling, source, place, senders):
    energies, _, width, _ = inverses.shape
    square = (width, width)
    outs = [pltpu.VMEM(square, BF)] * 2 + [pltpu.VMEM(square, F32), pltpu.HBM((2, *square), F32)]
    results = pl.pallas_call(
        functools.partial(prepare_kernel, senders),
        in_specs=[SMEM] + [HBM] * 3,
        out_specs=([VMEM] * 3 + [HBM]) * energies,
        out_shape=outs * energies,
        scratch_shapes=[
            pltpu.VMEM(inverses.shape, F32),
            pltpu.VMEM(coupling.shape, F32),
            pltpu.VMEM(source.shape, F32),
            pltpu.VMEM((energies, 2, 2, *square), F32),
            pltpu.VMEM((energies, 2, *square), F32),
            pltpu.SemaphoreType.DMA((2 + 4 * energies,)),
            pltpu.SemaphoreType.DMA((energies,)),
        ],
        compiler_params=params(16),
        cost_estimate=cost(18),
        name="prepare",
    )(place, *[far(a) for a in (inverses, coupling, source)])
    return [results[4 * e : 4 * e + 4] for e in range(energies)]


def through(pair, state):
    return sandwich(split(pair[0]), split(state)) + pair[1]


def hop_kernel(target, skips, place, entry, before, state, map_h, map_l, add, *refs):
    out, entry_out = refs[-2:]
    active = place[0] == target

    @pl.when(active)
    def _():
        begin = through(refs[0], state[...]) if skips else state[...]
        entry_out[...] = begin
        out[...] = sandwich((map_h[...], map_l[...]), split(begin)) + add[...]

    @pl.when(jnp.logical_not(active))
    def _():
        entry_out[...] = entry[...]
        out[...] = before[...]


def hop(target, place, entry, before, state, given, pair=None, weight=2):
    operands = [place, entry, before, state, *given[:3]]
    if pair is not None:
        operands.append(pair)
    return pl.pallas_call(
        functools.partial(hop_kernel, target, pair is not None),
        in_specs=[SMEM] + [VMEM] * (len(operands) - 1),
        out_specs=[VMEM] * 2,
        out_shape=[pltpu.VMEM(state.shape, F32)] * 2,
        compiler_params=params(),
        cost_estimate=cost(weight),
        name="hop",
    )(*operands)


def first_kernel(inv_all, coup_all, src_all, out, inv, coup, src, kept, sem):
    energies = inv_all.shape[0]
    copies = [pltpu.make_async_copy(coup_all.at[0], coup, sem.at[0])]
    for e in range(energies):
        copies.append(pltpu.make_async_copy(inv_all.at[e, 0], inv.at[e], sem.at[1 + 2 * e]))
        copies.append(pltpu.make_async_copy(src_all.at[e, 0], src.at[e], sem.at[2 + 2 * e]))
    for copy in copies:
        copy.start()
    for copy in copies:
        copy.wait()
    right = split(coup[...])
    stores = []
    for e in range(energies):
        left = split(inv[e])
        kept[e, 0] = product(left, right)
        kept[e, 1] = sandwich(left, split(src[e]))
        stores.append(pltpu.make_async_copy(kept.at[e], out.at[e], sem.at[1 + 2 * energies + e]))
        stores[-1].start()
    for store in stores:
        store.wait()


def first_terms(inverses, coupling, source):
    energies, _, width, _ = inverses.shape
    square = (width, width)
    return pl.pallas_call(
        first_kernel,
        in_specs=[HBM] * 3,
        out_specs=HBM,
        out_shape=pltpu.HBM((energies, 2, *square), F32),
        scratch_shapes=[
            pltpu.VMEM((energies, *square), F32),
            pltpu.VMEM(square, F32),
            pltpu.VMEM((energies, *square), F32),
            pltpu.VMEM((energies, 2, *square), F32),
            pltpu.SemaphoreType.DMA((1 + 3 * energies,)),
        ],
        compiler_params=params(16),
        cost_estimate=cost(6),
        name="first_terms",
    )(*[far(a) for a in (inverses, coupling, source)])


def pick_kernel(energy, end, late, place, live, rows, entry, state, side, map_h, map_l, add, pair, *refs):
    first_all = refs[0]
    out, begin, block, picked, sem = refs[-5:]
    here = place[0]
    sideways = functools.reduce(jnp.logical_or, [here == z for z in late])
    fetch = pltpu.make_async_copy(first_all.at[energy], block, sem.at[0])
    fetch.start()

    @pl.when(here == end)
    def _():
        begin[...] = through(pair, state[...])

    @pl.when(sideways)
    def _():
        begin[...] = side[...]

    @pl.when(jnp.logical_not(jnp.logical_or(here == end, sideways)))
    def _():
        begin[...] = entry[...]

    width = entry.shape[1]
    slots = rows.shape[0]
    column = lax.broadcasted_iota(jnp.int32, (slots, 2 * width), 1)
    slot = lax.broadcasted_iota(jnp.int32, (slots, 2 * width), 0)
    chosen = jnp.where((column == rows[...]) & (slot < live[0]), 1.0, 0.0).astype(BF)
    start = split(begin[...])
    last = sandwich((map_h[...], map_l[...]), start) + add[...]
    fetch.wait()
    high, low = split(jnp.concatenate([sandwich(split(block[0]), start) + block[1], last], axis=0))
    dot = lambda a, b: jnp.dot(a, b, preferred_element_type=F32)
    stores = []
    half = slots // 2
    for n in range(2):
        rows_in, groups = slice(n * half, (n + 1) * half), pl.ds(n * half // 8, half // 8)
        picked[groups] = (dot(chosen[rows_in], high) + dot(chosen[rows_in], low)).reshape(half // 8, 8, width)
        stores.append(pltpu.make_async_copy(picked.at[groups], out.at[groups, energy], sem.at[1 + n]))
        stores[-1].start()
    for store in stores:
        store.wait()


def pick(energy, end, late, place, live, rows, entry, state, side, pair, given, first, before=None):
    width = entry.shape[1]
    slots = rows.shape[0]
    operands = [place, live, rows, *[near(a) for a in (entry, state, side, *given[:3], pair)]]
    specs = [SMEM, SMEM] + [VMEM] * (len(operands) - 2) + [HBM]
    operands.append(far(first))
    aliases = {}
    if before is not None:
        aliases = {len(operands): 0}
        operands.append(before)
        specs.append(HBM)
    return pl.pallas_call(
        functools.partial(pick_kernel, energy, end, late),
        in_specs=specs,
        out_specs=HBM,
        out_shape=pltpu.HBM((slots // 8, 2, 8, width), F32),
        scratch_shapes=[
            pltpu.VMEM((width, width), F32),
            pltpu.VMEM((2, width, width), F32),
            pltpu.VMEM((slots // 8, 8, width), F32),
            pltpu.SemaphoreType.DMA((3,)),
        ],
        input_output_aliases=aliases,
        compiler_params=params(12),
        cost_estimate=cost(8),
        name="pick",
    )(*operands)


def transforms(count):
    half = count // 2
    points = np.arange(count)
    waves = np.arange(half)
    angle = 2.0 * math.pi * ((waves[:, None] * points[None, :]) % count) / count
    forward = np.concatenate([np.cos(angle), -np.sin(angle)], axis=0)
    forward[half] = np.where(points % 2 == 0, 1.0, -1.0)
    weight = np.full(count, 2.0 / count)
    weight[[0, half]] = 1.0 / count
    return forward.astype(np.float32), (forward.T * weight[None, :]).astype(np.float32)


def stacked(matrix):
    return jnp.concatenate(split(jnp.asarray(matrix)), axis=0)


def transform(matrix, data):
    count = data.shape[0]
    high, low = split(data)
    dot = lambda a, b: jnp.dot(a, b, preferred_element_type=F32)
    both = dot(matrix, high)
    return both[:count] + (both[count:] + dot(matrix[:count], low))


def spectrum_kernel(fwd, data, out):
    columns = jnp.swapaxes(data[...], 0, 1)
    for j in range(columns.shape[0]):
        out[j] = transform(fwd[...], columns[j])


def spectrum(forward, data):
    count, group, width = data.shape
    return pl.pallas_call(
        spectrum_kernel,
        in_specs=[VMEM] * 2,
        out_specs=VMEM,
        out_shape=pltpu.VMEM((group, count, width), F32),
        compiler_params=params(),
        cost_estimate=cost(2),
        name="spectrum",
    )(forward, far(data))


def convolve_kernel(fwd, inv, data, other, out):
    half = data.shape[0] // 2
    single = lax.broadcasted_iota(jnp.int32, (half, data.shape[2]), 0) == 0
    columns = jnp.swapaxes(data[...], 0, 1)
    results = []
    for j in range(columns.shape[0]):
        left = transform(fwd[...], columns[j])
        right = other[j]
        real_a, imag_a = left[:half], left[half:]
        real_b, imag_b = right[:half], right[half:]
        real_p = real_a * real_b - jnp.where(single, 0.0, imag_a * imag_b)
        imag_p = jnp.where(single, imag_a * imag_b, real_a * imag_b + imag_a * real_b)
        results.append(transform(inv[...], jnp.concatenate([real_p, imag_p], axis=0)))
    out[...] = jnp.swapaxes(jnp.stack(results), 0, 1)


def convolve(forward, inverse, data, other):
    count, group, width = data.shape
    return pl.pallas_call(
        convolve_kernel,
        in_specs=[VMEM] * 4,
        out_specs=VMEM,
        out_shape=jax.ShapeDtypeStruct((count, group, width), F32),
        compiler_params=params(),
        cost_estimate=cost(4),
        name="convolve",
    )(forward, inverse, data, near(other))


def arrange_kernel(data, after, out, sem):
    del after
    copies = [pltpu.make_async_copy(data.at[e], out.at[:, e], sem.at[e]) for e in range(data.shape[0])]
    for copy in copies:
        copy.start()
    for copy in copies:
        copy.wait()


def arrange(data, after):
    energies, parts = data.shape[:2]
    return pl.pallas_call(
        arrange_kernel,
        in_specs=[VMEM, VMEM],
        out_specs=HBM,
        out_shape=pltpu.HBM((parts, energies, *data.shape[2:]), F32),
        scratch_shapes=[pltpu.SemaphoreType.DMA((energies,))],
        compiler_params=params(),
        cost_estimate=cost(0.1),
        name="arrange",
    )(data, after)


def exchange(chunks):
    return lax.all_to_all(chunks, "energy", split_axis=0, concat_axis=0, tiled=True)


def body(inverses, coupling, source, screened, kept_rows, live_count):
    energies, slots, width = screened.shape
    parts = lax.axis_size("energy")
    spaces = lax.axis_size("space")
    place = lax.axis_index("space").astype(jnp.int32).reshape(1)
    group = slots // parts
    count = energies * parts
    forward, inverse = [stacked(m) for m in transforms(count)]

    middle = spaces // 2
    direct = list(range(middle))
    odd = list(range(middle + 1, spaces, 2))
    path = direct + odd
    given = prepare(inverses, coupling, source, place, [z - 1 for z in odd])
    pairs = [lax.ppermute(given[e][3], "space", [(z - 1, z) for z in odd]) for e in range(energies)]
    outgoing = [given[e][2] for e in range(energies)]
    entry = [jnp.zeros((width, width), F32)] * energies
    state = [None] * energies
    for step, (here, target) in enumerate(zip(path[:-1], path[1:])):
        for e in range(energies):
            state[e] = lax.ppermute(outgoing[e], "space", [(here, target)])
            if target != path[-1]:
                pair = pairs[e] if target in odd else None
                weight = 200 if step in (2, 3) else 2
                outgoing[e], entry[e] = hop(target, place, entry[e], outgoing[e], state[e], given[e], pair, weight)
        if step == 1:
            chunks = arrange(screened.reshape(energies, parts, group, width), outgoing[-1])
    late = [z - 1 for z in odd]
    other = spectrum(forward, exchange(chunks).reshape(count, group, width))
    side = [lax.ppermute(outgoing[e], "space", [(path[path.index(z) - 1], z - 1) for z in odd]) for e in range(energies)]

    rows = kept_rows.reshape(slots, 1)
    first = first_terms(inverses, coupling, source)
    picked = None
    for e in range(energies):
        picked = pick(
            e, path[-1], late, place, live_count, rows, entry[e], state[e], side[e], pairs[e], given[e], first, picked
        )
    data = exchange(picked).reshape(count, group, width)
    sigma = convolve(forward, inverse, data, other)
    back = exchange(sigma.reshape(parts, energies, group, width))
    return back.swapaxes(0, 1).reshape(energies, slots, width)


def solution(mesh):
    return jax.shard_map(
        body,
        mesh=mesh,
        in_specs=(
            P("energy", "space", None, None),
            P("space", None, None),
            P("energy", "space", None, None),
            P("energy", "space", None),
            P("space"),
            P("space"),
        ),
        out_specs=P("energy", "space", None),
        check_vma=False,
    )
```
